32 devices in a mesh: groups: 2 (over y), ctx: 8 (over z, core), rep: 2 (over x), row: 1.
Axes of the slice: x: 2, y: 2, z: 4, core: 2. Of those that a mesh axis runs over, the one named last changes fastest.
Arguments:
- queries: bfloat16 [4, 128, 64, 128], P(None, ('groups', 'ctx', 'row'), 'rep'), parts along dimension 1, may hold values from -8 to 8
- new_keys: bfloat16 [4, 128, 8, 128], P(None, ('groups', 'ctx', 'row'), 'rep'), parts along dimension 1, may hold values from -4.5 to 4.5
- step_new_values: bfloat16 [4, 128, 8, 128], P(None, ('groups', 'ctx', 'row'), 'rep'), parts along dimension 1, may hold values from -6 to 6
- context_keys: bfloat16 [8, 8192, 128], P('rep', ('groups', 'ctx')), parts along dimension 1, may hold values from -6 to 6
- context_values: bfloat16 [8, 8192, 128], P('rep', ('groups', 'ctx')), parts along dimension 1, may hold values from -6 to 6
- cluster_centroid_keys: bfloat16 [8, 64, 128], P('rep', ('groups', 'ctx')), parts along dimension 1, may hold values from -4 to 4
- cluster_mean_values: bfloat16 [8, 64, 128], P('rep', ('groups', 'ctx')), parts along dimension 1, may hold values from -6 to 6
- cluster_page_slot: int32 [8, 64], P('rep', 'groups'), parts along dimension 1, may hold values from 0 to 31, each once within a row
- picks: int32 [128, 8, 16], P(('groups', 'ctx', 'row'), 'rep'), parts along dimension 0, may hold values from 0 to 31, all different within a row
Outputs:
- attention: bfloat16 [4, 128, 64, 128], P(None, ('groups', 'ctx', 'row'), 'rep'), parts along dimension 1
The draws below stay inside these ranges and needn't reach their ends.
There are 2 independent parts, one for each index of `groups`. The reference program is written for one: setup_inputs(seed, part) draws one part's arguments, and reference() takes and returns one part's arrays. A program takes and returns all parts, laid end to end along the dimension named above; each array names one. Nothing has to cross between parts.
Inputs may be any that keep to these rules, and one draw needn't show every extreme that they name: `picks`: for each row and key-value head, 16 different cluster ids. `cluster_page_slot`: for each key-value head, every cluster has its own page slot; slot p lies on context shard p // 4.
All inputs are finite; a program needn't handle non-finite values.
Results may differ from the reference program's by a relative error of at most 0.0027.
Values may be sent and summed in bfloat16 or wider, within the bound.
A program may use at most 64 MiB of HBM per device.

```python
import math
import jax
import jax.numpy as jnp
from jax import lax

QUERY_HEADS = 64
KEY_VALUE_HEADS = 8
HEAD_SIZE = 128
SPAN_PER_GROUPING = 128
PICKED_CLUSTERS = 16
DECODE_STEPS = 4
CL_DEV = 4
DECODE_ROWS = 64
CLUSTER_COUNT = 32
CONTEXT_LENGTH = 4096
N_CTX = 8


def draw_queries(key, part):
    base_offset = jax.random.fold_in(key, 3)
    value_rows = 2.0 * jax.random.truncated_normal(base_offset, -4.0, 4.0, (DECODE_STEPS, DECODE_ROWS, QUERY_HEADS, HEAD_SIZE), jnp.float32)
    return value_rows.astype(jnp.bfloat16)


def draw_new_keys(key, part):
    base_offset = jax.random.fold_in(key, 5)
    value_rows = jax.random.truncated_normal(base_offset, -4.5, 4.5, (DECODE_STEPS, DECODE_ROWS, KEY_VALUE_HEADS, HEAD_SIZE), jnp.float32)
    return value_rows.astype(jnp.bfloat16)


def draw_context_keys(key, part):
    base_offset = jax.random.fold_in(key, 7)
    value_rows = jax.random.truncated_normal(base_offset, -6.0, 6.0, (KEY_VALUE_HEADS, CONTEXT_LENGTH, HEAD_SIZE), jnp.float32)
    return value_rows.astype(jnp.bfloat16)


def block_levels(stream_key, shape, pieces, low, high):
    factor_of, own = 1.0, jax.random.fold_in(stream_key, 6)
    for axis_at, blocks in pieces:
        steps = jnp.exp(jax.random.uniform(jax.random.fold_in(own, axis_at), (blocks,), jnp.float32, low / len(pieces), high / len(pieces)))
        factor_of = factor_of * jnp.repeat(steps, shape[axis_at] // blocks).reshape([-1 if axis == axis_at else 1 for axis in range(len(shape))])
    return factor_of


def distinct(key, rows, number_of, top, lift):
    ranking = jax.random.permutation(jax.random.fold_in(key, 1), number_of)
    boost = ranking
    for power in range(3):
        boost = boost * boost // number_of
    boost = boost * lift // number_of
    lots = jax.random.randint(jax.random.fold_in(key, 2), (rows, number_of), 0, 4096) + boost
    holders = jax.random.permutation(jax.random.fold_in(key, 3), rows)[jnp.arange(number_of) % rows]
    lots = jnp.where(jnp.arange(rows)[:, None] == holders[None, :], 1 << 14, lots)
    merit = lots * number_of + jnp.arange(number_of)
    return lax.top_k(merit.astype(jnp.int32), top)[1].astype(jnp.int32)


def scatter_about(rng, extent, scale, reach, shards=(), kind=jnp.bfloat16):
    level = block_levels(rng, extent, shards, -0.22, 0.18) if shards else 1.0
    values = jax.random.normal(rng, extent, jnp.float32) * scale * level
    return jnp.minimum(jnp.maximum(values, -reach), reach).astype(kind)


def setup_inputs(seed: int = 0, part: int = 0) -> dict:
    key_list = jax.random.split(jax.random.key(seed), 10)
    part_splits = jax.random.split(jax.random.fold_in(key_list[9], part), 10)
    return {
        "queries": draw_queries(jax.random.fold_in(jax.random.fold_in(key_list[9], part), 71), part),
        "new_keys": draw_new_keys(jax.random.fold_in(jax.random.fold_in(key_list[9], part), 71), part),
        "step_new_values": scatter_about(part_splits[2], (DECODE_STEPS, DECODE_ROWS, KEY_VALUE_HEADS, HEAD_SIZE), 1.0, 6.0, ((1, 8), (2, 2))),
        "context_keys": draw_context_keys(jax.random.fold_in(jax.random.fold_in(key_list[9], part), 71), part),
        "context_values": scatter_about(part_splits[4], (KEY_VALUE_HEADS, CONTEXT_LENGTH, HEAD_SIZE), 1.0, 6.0, ((0, 2), (1, 8))),
        "cluster_centroid_keys": scatter_about(part_splits[5], (KEY_VALUE_HEADS, CLUSTER_COUNT, HEAD_SIZE), 0.6, 4.0, ((0, 2), (1, 8))),
        "cluster_mean_values": scatter_about(part_splits[6], (KEY_VALUE_HEADS, CLUSTER_COUNT, HEAD_SIZE), 1.0, 6.0, ((0, 2), (1, 8))),
        "cluster_page_slot": jax.vmap(lambda own: jax.random.permutation(own, CLUSTER_COUNT))(jax.random.split(part_splits[7], KEY_VALUE_HEADS)).reshape((KEY_VALUE_HEADS, CLUSTER_COUNT)).astype(jnp.int32),
        "picks": distinct(part_splits[8], DECODE_ROWS * KEY_VALUE_HEADS, CLUSTER_COUNT, PICKED_CLUSTERS, 8192).reshape((DECODE_ROWS, KEY_VALUE_HEADS, PICKED_CLUSTERS)),
    }


FLOOR_SCORE = -10000.0

def tail_block(queries, new_keys, step_new_values, logit_multiplier):
    num_steps, num_rows, num_heads, head_width = queries.shape
    kv_heads = new_keys.shape[2]
    grouped = queries.astype(jnp.float32).reshape(num_steps, num_rows, kv_heads, num_heads // kv_heads, head_width)
    scores = jnp.einsum('srhgd,trhd->srhgt', grouped, new_keys.astype(jnp.float32)) * logit_multiplier
    step_ids = jnp.arange(num_steps, dtype=jnp.int32)
    causal = (step_ids[None, :] <= step_ids[:, None])[:, None, None, None, :]
    block_top = lax.optimization_barrier(jnp.max(jnp.where(causal, scores, FLOOR_SCORE), axis=-1))
    weights = jnp.where(causal, jnp.exp(scores - block_top[..., None]), 0.0)
    sum_total = lax.optimization_barrier(jnp.sum(weights, axis=-1))
    rounded = weights.astype(jnp.bfloat16).astype(jnp.float32)
    tail_out = jnp.einsum('srhgt,trhd->srhgd', rounded, step_new_values.astype(jnp.float32))
    return (tail_out.reshape(num_steps, num_rows, num_heads, head_width), sum_total.reshape(num_steps, num_rows, num_heads), block_top.reshape(num_steps, num_rows, num_heads))

def reference(queries, new_keys, step_new_values, context_keys, context_values, cluster_centroid_keys, cluster_mean_values, cluster_page_slot, picks):
    logit_multiplier = 1.0 / math.sqrt(HEAD_SIZE)
    membership_log_weight = math.log(SPAN_PER_GROUPING)
    query_group_size = QUERY_HEADS // KEY_VALUE_HEADS
    span_tokens = CL_DEV * SPAN_PER_GROUPING
    cluster_ids = jnp.arange(CLUSTER_COUNT, dtype=jnp.int32)
    chosen_page_slot = jnp.take_along_axis(jnp.broadcast_to(cluster_page_slot[None], (DECODE_ROWS, KEY_VALUE_HEADS, CLUSTER_COUNT)), picks, axis=2)
    slot_used = jnp.any(chosen_page_slot[..., None] == cluster_ids, axis=2)
    cluster_used = jnp.any(picks[..., None] == cluster_ids, axis=2)
    tail_out, tail_total, tail_top = tail_block(queries, new_keys, step_new_values, logit_multiplier)
    results = []
    for step_index in range(DECODE_STEPS):
        head_outs, head_totals, head_tops = ([], [], [])
        for current_head_index in range(KEY_VALUE_HEADS):
            generation_probe_vectors = queries[step_index, :, current_head_index * query_group_size:(current_head_index + 1) * query_group_size, :].reshape(DECODE_ROWS * query_group_size, HEAD_SIZE)
            head_keys = context_keys[current_head_index]
            head_values = context_values[current_head_index]
            head_cents = cluster_centroid_keys[current_head_index]
            head_cvals = cluster_mean_values[current_head_index]
            head_slots = slot_used[:, current_head_index]
            head_clusters = cluster_used[:, current_head_index]

            def block_part(shard_index):
                first_token = (shard_index * span_tokens).astype(jnp.int32)
                first_cluster = (shard_index * CL_DEV).astype(jnp.int32)
                block_keys = lax.dynamic_slice_in_dim(head_keys, first_token, span_tokens, 0)
                block_values = lax.dynamic_slice_in_dim(head_values, first_token, span_tokens, 0)
                tile_prototype_vectors = lax.dynamic_slice_in_dim(head_cents, first_cluster, CL_DEV, 0)
                block_cvals = lax.dynamic_slice_in_dim(head_cvals, first_cluster, CL_DEV, 0)
                exact_mask = lax.dynamic_slice_in_dim(head_slots, first_cluster, CL_DEV, 1)[:, None, :, None]
                coarse_mask = jnp.logical_not(lax.dynamic_slice_in_dim(head_clusters, first_cluster, CL_DEV, 1))[:, None, :]
                exact_scores = jnp.dot(generation_probe_vectors, block_keys.T, preferred_element_type=jnp.float32) * logit_multiplier
                exact_scores = exact_scores.reshape(DECODE_ROWS, query_group_size, CL_DEV, SPAN_PER_GROUPING)
                prototype_logits = jnp.dot(generation_probe_vectors, tile_prototype_vectors.T, preferred_element_type=jnp.float32) * logit_multiplier + membership_log_weight
                prototype_logits = prototype_logits.reshape(DECODE_ROWS, query_group_size, CL_DEV)
                block_top = jnp.maximum(lax.optimization_barrier(jnp.max(jnp.where(exact_mask, exact_scores, FLOOR_SCORE), axis=(2, 3))), lax.optimization_barrier(jnp.max(jnp.where(coarse_mask, prototype_logits, FLOOR_SCORE), axis=2)))
                exact_weights = jnp.where(exact_mask, jnp.exp(exact_scores - block_top[:, :, None, None]), 0.0)
                coarse_weights = jnp.where(coarse_mask, jnp.exp(prototype_logits - block_top[:, :, None]), 0.0)
                sum_total = lax.optimization_barrier(jnp.sum(exact_weights, axis=(2, 3))) + lax.optimization_barrier(jnp.sum(coarse_weights, axis=2))
                block_out = jnp.dot(exact_weights.astype(jnp.bfloat16).reshape(DECODE_ROWS * query_group_size, span_tokens), block_values, preferred_element_type=jnp.float32)
                block_out = block_out + jnp.dot(coarse_weights.astype(jnp.bfloat16).reshape(DECODE_ROWS * query_group_size, CL_DEV), block_cvals, preferred_element_type=jnp.float32)
                return (block_out.reshape(DECODE_ROWS, query_group_size, HEAD_SIZE), sum_total, block_top)
            partial_outs, partial_totals, partial_tops = lax.map(block_part, jnp.arange(N_CTX, dtype=jnp.int32))
            best_top = lax.optimization_barrier(jnp.max(partial_tops, axis=0))
            factor = jnp.exp(partial_tops - best_top)
            head_outs.append(lax.optimization_barrier(jnp.sum(factor[..., None] * partial_outs, axis=0)))
            head_totals.append(lax.optimization_barrier(jnp.sum(factor * partial_totals, axis=0)))
            head_tops.append(best_top)
        merged = jnp.concatenate(head_outs, axis=1)
        sum_total = jnp.concatenate(head_totals, axis=1)
        best_top = jnp.concatenate(head_tops, axis=1)
        overall = jnp.maximum(best_top, tail_top[step_index])
        context_factor = jnp.exp(best_top - overall)
        tail_factor = jnp.exp(tail_top[step_index] - overall)
        numer = context_factor[..., None] * merged + tail_factor[..., None] * tail_out[step_index]
        denom = context_factor * sum_total + tail_factor * tail_total[step_index]
        results.append(numer / denom[..., None])
    return jnp.stack(results).astype(jnp.bfloat16)
```

```python
import functools
import math

import jax
import jax.numpy as jnp
from jax import lax
from jax.experimental import pallas as pl
from jax.experimental.pallas import tpu as pltpu
from jax.sharding import PartitionSpec as P

FLOOR_SCORE = -10000.0


def tail_block(queries, new_keys, step_new_values, logit_multiplier):
    num_steps, num_rows, num_heads, head_width = queries.shape
    kv_heads = new_keys.shape[2]
    grouped = queries.astype(jnp.float32).reshape(
        num_steps, num_rows, kv_heads, num_heads // kv_heads, head_width
    )
    scores = (
        jnp.einsum("srhgd,trhd->srhgt", grouped, new_keys.astype(jnp.float32)) * logit_multiplier
    )
    step_ids = jnp.arange(num_steps, dtype=jnp.int32)
    causal = (step_ids[None, :] <= step_ids[:, None])[:, None, None, None, :]
    block_top = jnp.max(jnp.where(causal, scores, FLOOR_SCORE), axis=-1)
    weights = jnp.where(causal, jnp.exp(scores - block_top[..., None]), 0.0)
    sum_total = jnp.sum(weights, axis=-1)
    rounded = weights.astype(jnp.bfloat16).astype(jnp.float32)
    tail_out = jnp.einsum("srhgt,trhd->srhgd", rounded, step_new_values.astype(jnp.float32))
    return (
        tail_out.reshape(num_steps, num_rows, num_heads, head_width),
        sum_total.reshape(num_steps, num_rows, num_heads),
        block_top.reshape(num_steps, num_rows, num_heads),
    )


def per_device_plain(
    queries,
    new_keys,
    step_new_values,
    context_keys,
    context_values,
    cluster_centroid_keys,
    cluster_mean_values,
    cluster_page_slot,
    picks,
):
    num_steps = queries.shape[0]
    num_heads = queries.shape[2]
    head_width = queries.shape[3]
    kv_local = context_keys.shape[0]
    span_tokens = context_keys.shape[1]
    cl_local = cluster_centroid_keys.shape[1]
    grouping_member_entries = span_tokens // cl_local
    query_group_size = num_heads // kv_local
    logit_multiplier = 1.0 / math.sqrt(head_width)
    membership_log_weight = math.log(grouping_member_entries)
    shard_index = lax.axis_index("ctx")
    gathered = lax.all_gather(queries, "ctx", axis=1, tiled=True)
    chosen = lax.all_gather(picks, "ctx", axis=0, tiled=True)
    rows_all = gathered.shape[1]
    cluster_ids = jnp.arange(cluster_page_slot.shape[1], dtype=jnp.int32)
    pick_hits = chosen[..., None] == cluster_ids
    picked_slots = jnp.sum(jnp.where(pick_hits, cluster_page_slot[None, :, None, :], 0), axis=-1)
    local_ids = shard_index * cl_local + jnp.arange(cl_local, dtype=jnp.int32)
    slot_used = jnp.any(picked_slots[..., None] == local_ids, axis=2)
    cluster_used = jnp.any(chosen[..., None] == local_ids, axis=2)
    step_outs, step_totals, step_tops = ([], [], [])
    for step_index in range(num_steps):
        head_outs, head_totals, head_tops = ([], [], [])
        for current_head_index in range(kv_local):
            generation_probe_vectors = gathered[
                step_index,
                :,
                current_head_index * query_group_size : (current_head_index + 1) * query_group_size,
                :,
            ].reshape(rows_all * query_group_size, head_width)
            exact_mask = slot_used[:, current_head_index][:, None, :, None]
            coarse_mask = jnp.logical_not(cluster_used[:, current_head_index])[:, None, :]
            exact_scores = (
                jnp.einsum(
                    "qd,kd->qk",
                    generation_probe_vectors,
                    context_keys[current_head_index],
                    preferred_element_type=jnp.float32,
                )
                * logit_multiplier
            )
            exact_scores = exact_scores.reshape(
                rows_all, query_group_size, cl_local, grouping_member_entries
            )
            prototype_logits = (
                jnp.einsum(
                    "qd,kd->qk",
                    generation_probe_vectors,
                    cluster_centroid_keys[current_head_index],
                    preferred_element_type=jnp.float32,
                )
                * logit_multiplier
                + membership_log_weight
            )
            prototype_logits = prototype_logits.reshape(rows_all, query_group_size, cl_local)
            block_top = jnp.maximum(
                jnp.max(jnp.where(exact_mask, exact_scores, FLOOR_SCORE), axis=(2, 3)),
                jnp.max(jnp.where(coarse_mask, prototype_logits, FLOOR_SCORE), axis=2),
            )
            exact_weights = jnp.where(
                exact_mask, jnp.exp(exact_scores - block_top[:, :, None, None]), 0.0
            )
            coarse_weights = jnp.where(
                coarse_mask, jnp.exp(prototype_logits - block_top[:, :, None]), 0.0
            )
            sum_total = jnp.sum(exact_weights, axis=(2, 3)) + jnp.sum(coarse_weights, axis=2)
            block_out = jnp.dot(
                exact_weights.astype(jnp.bfloat16).reshape(
                    rows_all * query_group_size, span_tokens
                ),
                context_values[current_head_index],
                preferred_element_type=jnp.float32,
            )
            block_out = block_out + jnp.dot(
                coarse_weights.astype(jnp.bfloat16).reshape(rows_all * query_group_size, cl_local),
                cluster_mean_values[current_head_index],
                preferred_element_type=jnp.float32,
            )
            head_outs.append(block_out.reshape(rows_all, query_group_size, head_width))
            head_totals.append(sum_total)
            head_tops.append(block_top)
        step_outs.append(jnp.concatenate(head_outs, axis=1))
        step_totals.append(jnp.concatenate(head_totals, axis=1))
        step_tops.append(jnp.concatenate(head_tops, axis=1))
    partial_outs = jnp.stack(step_outs)
    partial_totals = jnp.stack(step_totals)
    partial_tops = jnp.stack(step_tops)
    got_tops, got_totals, got_outs = (
        lax.all_to_all(partial_tops[None], "ctx", split_axis=2, concat_axis=0, tiled=True),
        lax.all_to_all(partial_totals[None], "ctx", split_axis=2, concat_axis=0, tiled=True),
        lax.all_to_all(partial_outs[None], "ctx", split_axis=2, concat_axis=0, tiled=True),
    )
    best_top = jnp.max(got_tops, axis=0)
    factor = jnp.exp(got_tops - best_top)
    sum_total = jnp.sum(factor * got_totals, axis=0)
    merged = jnp.sum(factor[..., None] * got_outs, axis=0)
    tail_out, tail_total, tail_top = tail_block(
        queries, new_keys, step_new_values, logit_multiplier
    )
    overall = jnp.maximum(best_top, tail_top)
    context_factor = jnp.exp(best_top - overall)
    tail_factor = jnp.exp(tail_top - overall)
    numer = context_factor[..., None] * merged + tail_factor[..., None] * tail_out
    denom = context_factor * sum_total + tail_factor * tail_total
    return (numer / denom[..., None]).astype(jnp.bfloat16)


MESH = pl.DeviceIdType.MESH
LOG2E = math.log2(math.e)
NT = (((1,), (1,)), ((), ()))
TN = (((0,), (0,)), ((), ()))


def chain_kernel(
    n, dims,
    qx, kx, vx, nk, nv, out,
    qbuf, kb, vb, part, part_st, inc, inc_st, snd, snd_st, fin, fin_st, sib, sib_st,
    tail, tail_st, acc, acc_st, wbuf, score,
    q_send, f_send, q_recv, s_send, s_recv, f_recv, b_send, b_recv, kv_send, kv_recv,
):
    num_steps, rows, group, hh, cl, page, head_width, mask_groups = dims
    nq = num_steps * rows * group
    units = 2 * hh
    me = lax.axis_index("ctx")
    z, c = me // 2, me % 2
    o = 1 - c
    first, last = z == 0, z == n - 1
    scale2 = LOG2E / math.sqrt(head_width)
    coarse2 = LOG2E * math.log(page)
    floor2 = FLOOR_SCORE * LOG2E
    tokens = cl * page

    def copy(src, dst, send, recv, chip, core):
        return pltpu.make_async_remote_copy(
            src_ref=src, dst_ref=dst, send_sem=send, recv_sem=recv,
            device_id={"ctx": chip * 2 + core}, device_id_type=MESH,
        )

    barrier = pltpu.get_barrier_semaphore()
    pl.semaphore_signal(barrier, inc=1, device_id={"ctx": z * 2 + o}, device_id_type=MESH)

    @pl.when(jnp.logical_not(first))
    def _():
        for core in range(2):
            pl.semaphore_signal(barrier, inc=1, device_id={"ctx": (z - 1) * 2 + core}, device_id_type=MESH)

    @pl.when(jnp.logical_not(last))
    def _():
        for core in range(2):
            pl.semaphore_signal(barrier, inc=1, device_id={"ctx": (z + 1) * 2 + core}, device_id_type=MESH)

    pl.semaphore_wait(barrier, 5 - 2 * first.astype(jnp.int32) - 2 * last.astype(jnp.int32))

    def q_out(way, half, h):
        chip = (z - 1, z, z + 1)[way]
        return copy(qx.at[half, h], qbuf.at[z, c, h], q_send.at[way, half, h], q_recv.at[z, c, h], chip, half)

    def q_hop(b, sc, h, chip):
        ref = qbuf.at[b, sc, h]
        return copy(ref, ref, f_send.at[b, sc, h], q_recv.at[b, sc, h], chip, c)

    def kv_out():
        return (
            copy(kx.at[o], kb.at[c], kv_send.at[0], kv_recv.at[0], z, o),
            copy(vx.at[o], vb.at[c], kv_send.at[1], kv_recv.at[1], z, o),
        )

    for h in range(hh):
        q_out(1, o, h).start()

        @pl.when(jnp.logical_not(first))
        def _():
            for half in range(2):
                q_out(0, half, h).start()

        @pl.when(jnp.logical_not(last))
        def _():
            for half in range(2):
                q_out(2, half, h).start()

    for one in kv_out():
        one.start()

    kb[c] = kx[c]
    vb[c] = vx[c]
    qbuf[z, c] = qx[c]
    wbuf[...] = jnp.zeros_like(wbuf)

    def iota(shape, axis):
        return lax.broadcasted_iota(jnp.int32, shape, axis)

    def tail_head(hd, carry):
        q = qx[hd // hh, hd % hh, 0:nq, :]
        s = lax.dot_general(nk[hd], q, NT, preferred_element_type=jnp.float32) * scale2
        shape = (num_steps * rows, nq)
        t, r = iota(shape, 0) // rows, iota(shape, 0) % rows
        lane = iota(shape, 1)
        seen = jnp.logical_and((lane // group) % rows == r, t <= lane // (rows * group))
        s = jnp.where(seen, s, floor2)
        top = jnp.max(s, axis=0, keepdims=True)
        w = jnp.where(seen, jnp.exp2(s - top), 0.0)
        tail_st[hd, 0:1, :] = top
        tail_st[hd, 1:2, :] = jnp.sum(w, axis=0, keepdims=True)
        tail[hd] = lax.dot_general(nv[hd], w.astype(jnp.bfloat16), TN, preferred_element_type=jnp.float32)
        return carry

    lax.fori_loop(0, 2 * hh, tail_head, 0)

    sel_rows = 48
    si, sl = iota((sel_rows, 128), 0), iota((sel_rows, 128), 1)
    ncl = 2 * n * cl
    in_page = si < 2 * cl
    blk = jnp.where(si >= 32, 1, 0)
    j = si - 16 - 16 * blk
    in_coarse = jnp.logical_and(si >= 16, j < cl)
    target = jnp.where(in_page, z * 2 * cl + si, jnp.where(in_coarse, ncl + (z * 2 + blk) * cl + j, -1))
    spread = jnp.where((iota((16, nq), 1) // group) % rows == iota((16, nq), 0), 1.0, 0.0).astype(jnp.bfloat16)

    for one in kv_out():
        one.wait_recv()

    def compute(b, sc, h):
        q = qbuf[b, sc, h, 0:nq, :]
        flags = None
        for m in range(mask_groups):
            sel = jnp.where(sl + m * 128 == target, 1.0, 0.0).astype(jnp.bfloat16)
            bits = qbuf[b, sc, h, nq + 16 * m : nq + 16 * (m + 1), :]
            got = lax.dot_general(sel, bits, NT, preferred_element_type=jnp.float32)
            flags = got if flags is None else flags + got
        flags = jnp.dot(flags.astype(jnp.bfloat16), spread, preferred_element_type=jnp.float32)
        outs = []
        for d in range(2):
            score[...] = lax.dot_general(kb[d, h], q, NT, preferred_element_type=jnp.float32) * scale2
            coarse_on = flags[16 + 16 * d : 32 + 16 * d, :] > 0.5
            coarse = score[tokens : tokens + 16, :] + coarse2
            top = jnp.max(jnp.where(coarse_on, coarse, floor2), axis=0, keepdims=True)
            on = [flags[d * cl + p : d * cl + p + 1, :] > 0.5 for p in range(cl)]
            for p in range(cl):
                page_top = jnp.max(score[p * page : (p + 1) * page, :], axis=0, keepdims=True)
                top = jnp.maximum(top, jnp.where(on[p], page_top, floor2))
            wc = jnp.where(coarse_on, jnp.exp2(coarse - top), 0.0)
            wbuf[tokens : tokens + 16, :] = wc.astype(jnp.bfloat16)
            total = jnp.sum(wc, axis=0, keepdims=True)
            for p in range(cl):
                w = jnp.exp2(score[p * page : (p + 1) * page, :] - jnp.where(on[p], top, 1e30))
                wbuf[p * page : (p + 1) * page, :] = w.astype(jnp.bfloat16)
                total = total + jnp.sum(w, axis=0, keepdims=True)
            outs.append((jnp.dot(vb[d, h], wbuf[...], preferred_element_type=jnp.float32), total, top))
        (o0, l0, m0), (o1, l1, m1) = outs
        top = jnp.maximum(m0, m1)
        a0, a1 = jnp.exp2(m0 - top), jnp.exp2(m1 - top)
        part[b, sc, h] = a0 * o0 + a1 * o1
        part_st[b, sc, h, 0:1, :] = top
        part_st[b, sc, h, 1:2, :] = a0 * l0 + a1 * l1

    def merge(o_ref, st_ref, values, st):
        m0, m1 = st_ref[0:1, :], st[0:1, :]
        top = jnp.maximum(m0, m1)
        a0, a1 = jnp.exp2(m0 - top), jnp.exp2(m1 - top)
        o_ref[...] = a0 * o_ref[...] + a1 * values
        st_ref[1:2, :] = a0 * st_ref[1:2, :] + a1 * st[1:2, :]
        st_ref[0:1, :] = top

    def decode(ref, st_ref):
        return ref[...].astype(jnp.int32).astype(jnp.float32) * st_ref[2:3, :]

    def flow_out(b, sc, h, chip, way):
        def hop(fn):
            fn(
                copy(snd.at[b, sc, h], inc.at[b, sc, h], s_send.at[0, b, sc, h], s_recv.at[0, b, sc, h], chip, c),
                copy(snd_st.at[b, sc, h], inc_st.at[b, sc, h], s_send.at[1, b, sc, h], s_recv.at[1, b, sc, h], chip, c),
            )

        def home(fn):
            fn(
                copy(snd.at[b, sc, h], fin.at[way, c, h], s_send.at[0, b, sc, h], f_recv.at[0, way, c, h], b, sc),
                copy(snd_st.at[b, sc, h], fin_st.at[way, c, h], s_send.at[1, b, sc, h], f_recv.at[1, way, c, h], b, sc),
            )

        return hop, home

    def both_start(x, y):
        x.start()
        y.start()

    def both_wait_send(x, y):
        x.wait_send()
        y.wait_send()

    def both_wait_recv(x, y):
        x.wait_recv()
        y.wait_recv()

    def sib_out(h):
        return (
            copy(part.at[z, o, h], sib.at[h], b_send.at[0, h], b_recv.at[0, h], z, o),
            copy(part_st.at[z, o, h], sib_st.at[h], b_send.at[1, h], b_recv.at[1, h], z, o),
        )

    def step(i, carry):
        dist = i // (2 * units)
        u = (i // 2) % units
        side = i % 2
        sc = (u // hh + c) % 2
        h = u % hh
        b = z + (2 * side - 1) * dist
        valid = jnp.logical_and(jnp.logical_and(b >= 0, b < n), jnp.logical_or(dist > 0, side == 0))

        @pl.when(valid)
        def _():
            bb = jnp.clip(b, 0, n - 1)

            @pl.when(jnp.logical_or(dist > 0, sc != c))
            def _():
                q_hop(bb, sc, h, z).wait_recv()

            @pl.when(jnp.logical_and(bb < z, jnp.logical_not(last)))
            def _():
                q_hop(bb, sc, h, z + 1).start()

            @pl.when(jnp.logical_and(bb > z, jnp.logical_not(first)))
            def _():
                q_hop(bb, sc, h, z - 1).start()

            compute(bb, sc, h)

            @pl.when(jnp.logical_and(bb == z, sc != c))
            def _():
                both_start(*sib_out(h))

        bm = jnp.where(side == 0, 2 * (n - 1) - z - dist, dist - z)
        flows = jnp.where(
            side == 0, jnp.logical_and(bm >= 0, bm < z), jnp.logical_and(bm > z, bm < n)
        )

        @pl.when(flows)
        def _():
            bb = jnp.clip(bm, 0, n - 1)
            o_ref, st_ref = part.at[bb, sc, h], part_st.at[bb, sc, h]

            @pl.when(jnp.where(side == 0, jnp.logical_not(last), jnp.logical_not(first)))
            def _():
                flow_out(bb, sc, h, z, side)[0](both_wait_recv)
                merge(o_ref, st_ref, decode(inc.at[bb, sc, h], inc_st.at[bb, sc, h]), inc_st.at[bb, sc, h])

            values = o_ref[...]
            size = jnp.max(jnp.abs(values), axis=0, keepdims=True)
            fit = 32767.0 / jnp.maximum(size, 1e-30)
            snd[bb, sc, h] = jnp.round(values * fit).astype(jnp.int32).astype(jnp.int16)
            snd_st[bb, sc, h, 0:2, :] = st_ref[0:2, :]
            snd_st[bb, sc, h, 2:3, :] = jnp.maximum(size, 1e-30) * (1.0 / 32767.0)
            chip = z + 2 * side - 1
            hop, home = flow_out(bb, sc, h, chip, side)

            @pl.when(chip == bb)
            def _():
                home(both_start)

            @pl.when(chip != bb)
            def _():
                hop(both_start)

        return carry

    lax.fori_loop(0, (2 * n - 1) * 2 * units, step, 0)

    def finish(i, carry):
        half = (i // hh + c) % 2
        h = i % hh
        hd = half * hh + h
        acc[...] = tail[hd]
        acc_st[...] = tail_st[hd]

        @pl.when(half == c)
        def _():
            merge(acc, acc_st, part[z, c, h], part_st.at[z, c, h])

        @pl.when(half != c)
        def _():
            both_wait_recv(*sib_out(h))
            merge(acc, acc_st, sib[h], sib_st.at[h])

        def arrive(way):
            both_wait_recv(
                copy(snd.at[0, 0, 0], fin.at[way, half, h], s_send.at[0, 0, 0, 0], f_recv.at[0, way, half, h], z, c),
                copy(snd_st.at[0, 0, 0], fin_st.at[way, half, h], s_send.at[1, 0, 0, 0], f_recv.at[1, way, half, h], z, c),
            )
            merge(acc, acc_st, decode(fin.at[way, half, h], fin_st.at[way, half, h]), fin_st.at[way, half, h])

        @pl.when(jnp.logical_not(last))
        def _():
            arrive(0)

        @pl.when(jnp.logical_not(first))
        def _():
            arrive(1)

        out[hd] = jnp.transpose(acc[...] / acc_st[1:2, :]).astype(jnp.bfloat16)
        return carry

    lax.fori_loop(0, units, finish, 0)

    for one in kv_out():
        one.wait_send()
    for h in range(hh):
        both_wait_send(*sib_out(h))
        q_out(1, o, h).wait_send()

        @pl.when(jnp.logical_not(first))
        def _():
            for half in range(2):
                q_out(0, half, h).wait_send()

        @pl.when(jnp.logical_not(last))
        def _():
            for half in range(2):
                q_out(2, half, h).wait_send()

    def drain(i, carry):
        b, sc, h = i // units, (i // hh) % 2, i % hh

        @pl.when(b != z)
        def _():
            flow_out(b, sc, h, z, 0)[0](both_wait_send)

            @pl.when(jnp.where(b < z, jnp.logical_not(last), jnp.logical_not(first)))
            def _():
                q_hop(b, sc, h, z).wait_send()

        return carry

    lax.fori_loop(0, n * units, drain, 0)


def per_device_paired(
    n,
    queries,
    new_keys,
    step_new_values,
    context_keys,
    context_values,
    cluster_centroid_keys,
    cluster_mean_values,
    cluster_page_slot,
    picks,
):
    num_steps, rows, num_heads, head_width = queries.shape
    kv_local, tokens = context_keys.shape[:2]
    cl = cluster_centroid_keys.shape[1]
    ncl = cluster_page_slot.shape[1]
    page = tokens // cl
    group = num_heads // kv_local
    hh = kv_local // 2
    nq = num_steps * rows * group
    bf16, f32, i16 = jnp.bfloat16, jnp.float32, jnp.int16
    q = queries.reshape(num_steps, rows, kv_local, group, head_width)
    q = q.transpose(2, 0, 1, 3, 4).reshape(2, hh, nq, head_width)
    ids = jnp.arange(ncl, dtype=jnp.int32)
    used = jnp.any(picks[..., None] == ids, axis=2)
    slots = jnp.any(
        jnp.logical_and(used[..., None], cluster_page_slot[None, :, :, None] == ids), axis=2
    )
    flags = jnp.concatenate([slots, jnp.logical_not(used)], axis=-1).astype(bf16)
    mask_groups = -(-2 * ncl // 128)
    flags = jnp.pad(flags.transpose(1, 0, 2), ((0, 0), (0, 16 - rows), (0, mask_groups * 128 - 2 * ncl)))
    flags = flags.reshape(kv_local, 16, mask_groups, 128).transpose(0, 2, 1, 3)
    flags = flags.reshape(2, hh, mask_groups * 16, 128)
    qx = jnp.concatenate([q, flags], axis=2)
    pad = ((0, 0), (0, 16 - cl), (0, 0))
    kx = jnp.concatenate([context_keys, jnp.pad(cluster_centroid_keys, pad)], axis=1)
    kx = kx.reshape(2, hh, tokens + 16, head_width)
    pad = ((0, 0), (0, 128 - cl), (0, 0))
    vx = jnp.concatenate([context_values, jnp.pad(cluster_mean_values, pad)], axis=1)
    vx = vx.transpose(0, 2, 1).reshape(2, hh, head_width, tokens + 128)
    nk = new_keys.transpose(2, 0, 1, 3).reshape(kv_local, num_steps * rows, head_width)
    nv = step_new_values.transpose(2, 0, 1, 3).reshape(kv_local, num_steps * rows, head_width)
    dims = (num_steps, rows, group, hh, cl, page, head_width, mask_groups)
    dma = pltpu.SemaphoreType.DMA
    vm = pltpu.VMEM
    unit = (n, 2, hh)
    out = pl.pallas_call(
        functools.partial(chain_kernel, n, dims),
        out_shape=jax.ShapeDtypeStruct((kv_local, nq, head_width), bf16),
        in_specs=[pl.BlockSpec(memory_space=pltpu.VMEM)] * 5,
        out_specs=pl.BlockSpec(memory_space=pltpu.VMEM),
        scratch_shapes=[
            vm(unit + qx.shape[2:], bf16),
            vm(kx.shape, bf16),
            vm(vx.shape, bf16),
            vm(unit + (head_width, nq), f32),
            vm(unit + (4, nq), f32),
            vm(unit + (head_width, nq), i16),
            vm(unit + (4, nq), f32),
            vm(unit + (head_width, nq), i16),
            vm(unit + (4, nq), f32),
            vm((2, 2, hh, head_width, nq), i16),
            vm((2, 2, hh, 4, nq), f32),
            vm((hh, head_width, nq), f32),
            vm((hh, 4, nq), f32),
            vm((kv_local, head_width, nq), f32),
            vm((kv_local, 4, nq), f32),
            vm((head_width, nq), f32),
            vm((4, nq), f32),
            vm((tokens + 128, nq), bf16),
            vm((tokens + 16, nq), f32),
            dma((3, 2, hh)),
            dma(unit),
            dma(unit),
            dma((2,) + unit),
            dma((2,) + unit),
            dma((2, 2, 2, hh)),
            dma((2, hh)),
            dma((2, hh)),
            dma((2,)),
            dma((2,)),
        ],
        compiler_params=pltpu.CompilerParams(
            collective_id=0, has_side_effects=True, vmem_limit_bytes=40 * 1024 * 1024
        ),
        cost_estimate=pl.CostEstimate(
            flops=8 * n * 2 * kv_local * nq * tokens * head_width,
            bytes_accessed=8 * 1024 * 1024,
            transcendentals=2 * n * kv_local * nq * tokens,
        ),
    )(qx, kx, vx, nk, nv)
    out = out.reshape(kv_local, num_steps, rows, group, head_width)
    return out.transpose(1, 2, 0, 3, 4).reshape(num_steps, rows, num_heads, head_width)


def solution(mesh):
    sizes = mesh.shape
    paired = sizes["row"] == 1 and sizes["ctx"] % 2 == 0
    step = functools.partial(per_device_paired, sizes["ctx"] // 2) if paired else per_device_plain
    return jax.shard_map(
        step,
        mesh=mesh,
        in_specs=(
            P(None, ("groups", "ctx", "row"), "rep", None),
            P(None, ("groups", "ctx", "row"), "rep", None),
            P(None, ("groups", "ctx", "row"), "rep", None),
            P("rep", ("groups", "ctx"), None),
            P("rep", ("groups", "ctx"), None),
            P("rep", ("groups", "ctx"), None),
            P("rep", ("groups", "ctx"), None),
            P("rep", "groups"),
            P(("groups", "ctx", "row"), "rep", None),
        ),
        out_specs=P(None, ("groups", "ctx", "row"), "rep", None),
        check_vma=False,
    )
```

```python
import functools
import math

import jax
import jax.numpy as jnp
from jax import lax
from jax.experimental import pallas as pl
from jax.experimental.pallas import tpu as pltpu
from jax.sharding import PartitionSpec as P

FLOOR_SCORE = -10000.0


def tail_block(queries, new_keys, step_new_values, logit_multiplier):
    num_steps, num_rows, num_heads, head_width = queries.shape
    kv_heads = new_keys.shape[2]
    grouped = queries.astype(jnp.float32).reshape(
        num_steps, num_rows, kv_heads, num_heads // kv_heads, head_width
    )
    scores = (
        jnp.einsum("srhgd,trhd->srhgt", grouped, new_keys.astype(jnp.float32)) * logit_multiplier
    )
    step_ids = jnp.arange(num_steps, dtype=jnp.int32)
    causal = (step_ids[None, :] <= step_ids[:, None])[:, None, None, None, :]
    block_top = jnp.max(jnp.where(causal, scores, FLOOR_SCORE), axis=-1)
    weights = jnp.where(causal, jnp.exp(scores - block_top[..., None]), 0.0)
    sum_total = jnp.sum(weights, axis=-1)
    rounded = weights.astype(jnp.bfloat16).astype(jnp.float32)
    tail_out = jnp.einsum("srhgt,trhd->srhgd", rounded, step_new_values.astype(jnp.float32))
    return (
        tail_out.reshape(num_steps, num_rows, num_heads, head_width),
        sum_total.reshape(num_steps, num_rows, num_heads),
        block_top.reshape(num_steps, num_rows, num_heads),
    )


def per_device_plain(
    queries,
    new_keys,
    step_new_values,
    context_keys,
    context_values,
    cluster_centroid_keys,
    cluster_mean_values,
    cluster_page_slot,
    picks,
):
    num_steps = queries.shape[0]
    num_heads = queries.shape[2]
    head_width = queries.shape[3]
    kv_local = context_keys.shape[0]
    span_tokens = context_keys.shape[1]
    cl_local = cluster_centroid_keys.shape[1]
    grouping_member_entries = span_tokens // cl_local
    query_group_size = num_heads // kv_local
    logit_multiplier = 1.0 / math.sqrt(head_width)
    membership_log_weight = math.log(grouping_member_entries)
    shard_index = lax.axis_index("ctx")
    gathered = lax.all_gather(queries, "ctx", axis=1, tiled=True)
    chosen = lax.all_gather(picks, "ctx", axis=0, tiled=True)
    rows_all = gathered.shape[1]
    cluster_ids = jnp.arange(cluster_page_slot.shape[1], dtype=jnp.int32)
    pick_hits = chosen[..., None] == cluster_ids
    picked_slots = jnp.sum(jnp.where(pick_hits, cluster_page_slot[None, :, None, :], 0), axis=-1)
    local_ids = shard_index * cl_local + jnp.arange(cl_local, dtype=jnp.int32)
    slot_used = jnp.any(picked_slots[..., None] == local_ids, axis=2)
    cluster_used = jnp.any(chosen[..., None] == local_ids, axis=2)
    step_outs, step_totals, step_tops = ([], [], [])
    for step_index in range(num_steps):
        head_outs, head_totals, head_tops = ([], [], [])
        for current_head_index in range(kv_local):
            generation_probe_vectors = gathered[
                step_index,
                :,
                current_head_index * query_group_size : (current_head_index + 1) * query_group_size,
                :,
            ].reshape(rows_all * query_group_size, head_width)
            exact_mask = slot_used[:, current_head_index][:, None, :, None]
            coarse_mask = jnp.logical_not(cluster_used[:, current_head_index])[:, None, :]
            exact_scores = (
                jnp.einsum(
                    "qd,kd->qk",
                    generation_probe_vectors,
                    context_keys[current_head_index],
                    preferred_element_type=jnp.float32,
                )
                * logit_multiplier
            )
            exact_scores = exact_scores.reshape(
                rows_all, query_group_size, cl_local, grouping_member_entries
            )
            prototype_logits = (
                jnp.einsum(
                    "qd,kd->qk",
                    generation_probe_vectors,
                    cluster_centroid_keys[current_head_index],
                    preferred_element_type=jnp.float32,
                )
                * logit_multiplier
                + membership_log_weight
            )
            prototype_logits = prototype_logits.reshape(rows_all, query_group_size, cl_local)
            block_top = jnp.maximum(
                jnp.max(jnp.where(exact_mask, exact_scores, FLOOR_SCORE), axis=(2, 3)),
                jnp.max(jnp.where(coarse_mask, prototype_logits, FLOOR_SCORE), axis=2),
            )
            exact_weights = jnp.where(
                exact_mask, jnp.exp(exact_scores - block_top[:, :, None, None]), 0.0
            )
            coarse_weights = jnp.where(
                coarse_mask, jnp.exp(prototype_logits - block_top[:, :, None]), 0.0
            )
            sum_total = jnp.sum(exact_weights, axis=(2, 3)) + jnp.sum(coarse_weights, axis=2)
            block_out = jnp.dot(
                exact_weights.astype(jnp.bfloat16).reshape(
                    rows_all * query_group_size, span_tokens
                ),
                context_values[current_head_index],
                preferred_element_type=jnp.float32,
            )
            block_out = block_out + jnp.dot(
                coarse_weights.astype(jnp.bfloat16).reshape(rows_all * query_group_size, cl_local),
                cluster_mean_values[current_head_index],
                preferred_element_type=jnp.float32,
            )
            head_outs.append(block_out.reshape(rows_all, query_group_size, head_width))
            head_totals.append(sum_total)
            head_tops.append(block_top)
        step_outs.append(jnp.concatenate(head_outs, axis=1))
        step_totals.append(jnp.concatenate(head_totals, axis=1))
        step_tops.append(jnp.concatenate(head_tops, axis=1))
    partial_outs = jnp.stack(step_outs)
    partial_totals = jnp.stack(step_totals)
    partial_tops = jnp.stack(step_tops)
    got_tops, got_totals, got_outs = (
        lax.all_to_all(partial_tops[None], "ctx", split_axis=2, concat_axis=0, tiled=True),
        lax.all_to_all(partial_totals[None], "ctx", split_axis=2, concat_axis=0, tiled=True),
        lax.all_to_all(partial_outs[None], "ctx", split_axis=2, concat_axis=0, tiled=True),
    )
    best_top = jnp.max(got_tops, axis=0)
    factor = jnp.exp(got_tops - best_top)
    sum_total = jnp.sum(factor * got_totals, axis=0)
    merged = jnp.sum(factor[..., None] * got_outs, axis=0)
    tail_out, tail_total, tail_top = tail_block(
        queries, new_keys, step_new_values, logit_multiplier
    )
    overall = jnp.maximum(best_top, tail_top)
    context_factor = jnp.exp(best_top - overall)
    tail_factor = jnp.exp(tail_top - overall)
    numer = context_factor[..., None] * merged + tail_factor[..., None] * tail_out
    denom = context_factor * sum_total + tail_factor * tail_total
    return (numer / denom[..., None]).astype(jnp.bfloat16)


MESH = pl.DeviceIdType.MESH
LOG2E = math.log2(math.e)
NT = (((1,), (1,)), ((), ()))
TN = (((0,), (0,)), ((), ()))


def chain_kernel(
    n, dims,
    qx, kx, vx, nk, nv, out,
    qbuf, kb, vb, part, part_st, inc, inc_st, snd, snd_st, fin, fin_st, sib, sib_st,
    tail, tail_st, acc, acc_st, wbuf, score,
    q_send, f_send, q_recv, s_send, s_recv, f_recv, b_send, b_recv, kv_send, kv_recv,
):
    num_steps, rows, group, hh, cl, page, head_width, mask_groups = dims
    nq = num_steps * rows * group
    units = 2 * hh
    me = lax.axis_index("ctx")
    z, c = me // 2, me % 2
    o = 1 - c
    first, last = z == 0, z == n - 1
    scale2 = LOG2E / math.sqrt(head_width)
    coarse2 = LOG2E * math.log(page)
    floor2 = FLOOR_SCORE * LOG2E
    tokens = cl * page

    def copy(src, dst, send, recv, chip, core):
        return pltpu.make_async_remote_copy(
            src_ref=src, dst_ref=dst, send_sem=send, recv_sem=recv,
            device_id={"ctx": chip * 2 + core}, device_id_type=MESH,
        )

    barrier = pltpu.get_barrier_semaphore()
    pl.semaphore_signal(barrier, inc=1, device_id={"ctx": z * 2 + o}, device_id_type=MESH)

    @pl.when(jnp.logical_not(first))
    def _():
        for core in range(2):
            pl.semaphore_signal(barrier, inc=1, device_id={"ctx": (z - 1) * 2 + core}, device_id_type=MESH)

    @pl.when(jnp.logical_not(last))
    def _():
        for core in range(2):
            pl.semaphore_signal(barrier, inc=1, device_id={"ctx": (z + 1) * 2 + core}, device_id_type=MESH)

    pl.semaphore_wait(barrier, 5 - 2 * first.astype(jnp.int32) - 2 * last.astype(jnp.int32))

    def q_out(way, half, h):
        chip = (z - 1, z, z + 1)[way]
        return copy(qx.at[half, h], qbuf.at[z, c, h], q_send.at[way, half, h], q_recv.at[z, c, h], chip, half)

    def q_hop(b, sc, h, chip):
        ref = qbuf.at[b, sc, h]
        return copy(ref, ref, f_send.at[b, sc, h], q_recv.at[b, sc, h], chip, c)

    def kv_out():
        return (
            copy(kx.at[o], kb.at[c], kv_send.at[0], kv_recv.at[0], z, o),
            copy(vx.at[o], vb.at[c], kv_send.at[1], kv_recv.at[1], z, o),
        )

    for h in range(hh):
        q_out(1, o, h).start()

        @pl.when(jnp.logical_not(first))
        def _():
            for half in range(2):
                q_out(0, half, h).start()

        @pl.when(jnp.logical_not(last))
        def _():
            for half in range(2):
                q_out(2, half, h).start()

    for one in kv_out():
        one.start()

    kb[c] = kx[c]
    vb[c] = vx[c]
    qbuf[z, c] = qx[c]
    wbuf[...] = jnp.zeros_like(wbuf)

    def iota(shape, axis):
        return lax.broadcasted_iota(jnp.int32, shape, axis)

    def tail_head(hd, carry):
        q = qx[hd // hh, hd % hh, 0:nq, :]
        s = lax.dot_general(nk[hd], q, NT, preferred_element_type=jnp.float32) * scale2
        shape = (num_steps * rows, nq)
        t, r = iota(shape, 0) // rows, iota(shape, 0) % rows
        lane = iota(shape, 1)
        seen = jnp.logical_and((lane // group) % rows == r, t <= lane // (rows * group))
        s = jnp.where(seen, s, floor2)
        top = jnp.max(s, axis=0, keepdims=True)
        w = jnp.where(seen, jnp.exp2(s - top), 0.0)
        tail_st[hd, 0:1, :] = top
        tail_st[hd, 1:2, :] = jnp.sum(w, axis=0, keepdims=True)
        tail[hd] = lax.dot_general(nv[hd], w.astype(jnp.bfloat16), TN, preferred_element_type=jnp.float32)
        return carry

    lax.fori_loop(0, 2 * hh, tail_head, 0)

    sel_rows = 48
    si, sl = iota((sel_rows, 128), 0), iota((sel_rows, 128), 1)
    ncl = 2 * n * cl
    in_page = si < 2 * cl
    blk = jnp.where(si >= 32, 1, 0)
    j = si - 16 - 16 * blk
    in_coarse = jnp.logical_and(si >= 16, j < cl)
    target = jnp.where(in_page, z * 2 * cl + si, jnp.where(in_coarse, ncl + (z * 2 + blk) * cl + j, -1))
    spread = jnp.where((iota((16, nq), 1) // group) % rows == iota((16, nq), 0), 1.0, 0.0).astype(jnp.bfloat16)

    for one in kv_out():
        one.wait_recv()

    def compute(b, sc, h):
        q = qbuf[b, sc, h, 0:nq, :]
        flags = None
        for m in range(mask_groups):
            sel = jnp.where(sl + m * 128 == target, 1.0, 0.0).astype(jnp.bfloat16)
            bits = qbuf[b, sc, h, nq + 16 * m : nq + 16 * (m + 1), :]
            got = lax.dot_general(sel, bits, NT, preferred_element_type=jnp.float32)
            flags = got if flags is None else flags + got
        flags = jnp.dot(flags.astype(jnp.bfloat16), spread, preferred_element_type=jnp.float32)
        outs = []
        for d in range(2):
            score[d] = lax.dot_general(kb[d, h], q, NT, preferred_element_type=jnp.float32) * scale2
        for d in range(2):
            coarse_on = flags[16 + 16 * d : 32 + 16 * d, :] > 0.5
            coarse = score[d, tokens : tokens + 16, :] + coarse2
            top = jnp.max(jnp.where(coarse_on, coarse, floor2), axis=0, keepdims=True)
            on = [flags[d * cl + p : d * cl + p + 1, :] > 0.5 for p in range(cl)]
            for p in range(cl):
                page_top = jnp.max(score[d, p * page : (p + 1) * page, :], axis=0, keepdims=True)
                top = jnp.maximum(top, jnp.where(on[p], page_top, floor2))
            wc = jnp.where(coarse_on, jnp.exp2(coarse - top), 0.0)
            wbuf[d, tokens : tokens + 16, :] = wc.astype(jnp.bfloat16)
            total = jnp.sum(wc, axis=0, keepdims=True)
            for p in range(cl):
                w = jnp.exp2(score[d, p * page : (p + 1) * page, :] - jnp.where(on[p], top, 1e30))
                wbuf[d, p * page : (p + 1) * page, :] = w.astype(jnp.bfloat16)
                total = total + jnp.sum(w, axis=0, keepdims=True)
            outs.append((jnp.dot(vb[d, h], wbuf[d], preferred_element_type=jnp.float32), total, top))
        (o0, l0, m0), (o1, l1, m1) = outs
        top = jnp.maximum(m0, m1)
        a0, a1 = jnp.exp2(m0 - top), jnp.exp2(m1 - top)
        part[b, sc, h] = a0 * o0 + a1 * o1
        part_st[b, sc, h, 0:1, :] = top
        part_st[b, sc, h, 1:2, :] = a0 * l0 + a1 * l1

    def merge(o_ref, st_ref, values, st):
        m0, m1 = st_ref[0:1, :], st[0:1, :]
        top = jnp.maximum(m0, m1)
        a0, a1 = jnp.exp2(m0 - top), jnp.exp2(m1 - top)
        o_ref[...] = a0 * o_ref[...] + a1 * values
        st_ref[1:2, :] = a0 * st_ref[1:2, :] + a1 * st[1:2, :]
        st_ref[0:1, :] = top

    def decode(ref, st_ref):
        return ref[...].astype(jnp.int32).astype(jnp.float32) * st_ref[2:3, :]

    def flow_out(b, sc, h, chip, way):
        def hop(fn):
            fn(
                copy(snd.at[b, sc, h], inc.at[b, sc, h], s_send.at[0, b, sc, h], s_recv.at[0, b, sc, h], chip, c),
                copy(snd_st.at[b, sc, h], inc_st.at[b, sc, h], s_send.at[1, b, sc, h], s_recv.at[1, b, sc, h], chip, c),
            )

        def home(fn):
            fn(
                copy(snd.at[b, sc, h], fin.at[way, c, h], s_send.at[0, b, sc, h], f_recv.at[0, way, c, h], b, sc),
                copy(snd_st.at[b, sc, h], fin_st.at[way, c, h], s_send.at[1, b, sc, h], f_recv.at[1, way, c, h], b, sc),
            )

        return hop, home

    def both_start(x, y):
        x.start()
        y.start()

    def both_wait_send(x, y):
        x.wait_send()
        y.wait_send()

    def both_wait_recv(x, y):
        x.wait_recv()
        y.wait_recv()

    def sib_out(h):
        return (
            copy(part.at[z, o, h], sib.at[h], b_send.at[0, h], b_recv.at[0, h], z, o),
            copy(part_st.at[z, o, h], sib_st.at[h], b_send.at[1, h], b_recv.at[1, h], z, o),
        )

    lead = hh

    def slot(i):
        dist = i // (2 * units)
        u = (i // 2) % units
        side = i % 2
        return dist, side, (u // hh + c) % 2, u % hh, z + (2 * side - 1) * dist, u

    def step(i, carry):
        dist, side, sc, h, b, _ = slot(i + 2 * lead)

        @pl.when(jnp.logical_and(dist > 0, jnp.logical_and(b >= 0, b < n)))
        def _():
            bb = jnp.clip(b, 0, n - 1)
            q_hop(bb, sc, h, z).wait_recv()

            @pl.when(jnp.logical_and(bb < z, jnp.logical_not(last)))
            def _():
                q_hop(bb, sc, h, z + 1).start()

            @pl.when(jnp.logical_and(bb > z, jnp.logical_not(first)))
            def _():
                q_hop(bb, sc, h, z - 1).start()

        dist, side, sc, h, b, u = slot(i)
        b = jnp.where(dist == n, z, b)
        valid = jnp.where(
            dist % n == 0,
            jnp.logical_and(side == 0, jnp.where(dist == 0, u < hh, jnp.logical_and(dist == n, u >= hh))),
            jnp.logical_and(b >= 0, b < n),
        )

        @pl.when(valid)
        def _():
            bb = jnp.clip(b, 0, n - 1)

            @pl.when(jnp.logical_and(bb == z, sc != c))
            def _():
                q_hop(bb, sc, h, z).wait_recv()

            compute(bb, sc, h)

            @pl.when(jnp.logical_and(bb == z, sc != c))
            def _():
                both_start(*sib_out(h))

        bm = jnp.where(side == 0, 2 * (n - 1) - z - dist, dist - z)
        flows = jnp.where(
            side == 0, jnp.logical_and(bm >= 0, bm < z), jnp.logical_and(bm > z, bm < n)
        )

        @pl.when(flows)
        def _():
            bb = jnp.clip(bm, 0, n - 1)
            o_ref, st_ref = part.at[bb, sc, h], part_st.at[bb, sc, h]

            @pl.when(jnp.where(side == 0, jnp.logical_not(last), jnp.logical_not(first)))
            def _():
                flow_out(bb, sc, h, z, side)[0](both_wait_recv)
                merge(o_ref, st_ref, decode(inc.at[bb, sc, h], inc_st.at[bb, sc, h]), inc_st.at[bb, sc, h])

            values = o_ref[...]
            size = jnp.max(jnp.abs(values), axis=0, keepdims=True)
            fit = 32767.0 / jnp.maximum(size, 1e-30)
            snd[bb, sc, h] = jnp.round(values * fit).astype(jnp.int32).astype(jnp.int16)
            snd_st[bb, sc, h, 0:2, :] = st_ref[0:2, :]
            snd_st[bb, sc, h, 2:3, :] = jnp.maximum(size, 1e-30) * (1.0 / 32767.0)
            chip = z + 2 * side - 1
            hop, home = flow_out(bb, sc, h, chip, side)

            @pl.when(chip == bb)
            def _():
                home(both_start)

            @pl.when(chip != bb)
            def _():
                hop(both_start)

        return carry

    lax.fori_loop(0, (2 * n - 1) * 2 * units, step, 0)

    def finish(i, carry):
        half = (i // hh + c) % 2
        h = i % hh
        hd = half * hh + h
        acc[...] = tail[hd]
        acc_st[...] = tail_st[hd]

        @pl.when(half == c)
        def _():
            merge(acc, acc_st, part[z, c, h], part_st.at[z, c, h])

        @pl.when(half != c)
        def _():
            both_wait_recv(*sib_out(h))
            merge(acc, acc_st, sib[h], sib_st.at[h])

        def arrive(way):
            both_wait_recv(
                copy(snd.at[0, 0, 0], fin.at[way, half, h], s_send.at[0, 0, 0, 0], f_recv.at[0, way, half, h], z, c),
                copy(snd_st.at[0, 0, 0], fin_st.at[way, half, h], s_send.at[1, 0, 0, 0], f_recv.at[1, way, half, h], z, c),
            )
            merge(acc, acc_st, decode(fin.at[way, half, h], fin_st.at[way, half, h]), fin_st.at[way, half, h])

        @pl.when(jnp.logical_not(last))
        def _():
            arrive(0)

        @pl.when(jnp.logical_not(first))
        def _():
            arrive(1)

        out[hd] = jnp.transpose(acc[...] / acc_st[1:2, :]).astype(jnp.bfloat16)
        return carry

    lax.fori_loop(0, units, finish, 0)

    for one in kv_out():
        one.wait_send()
    for h in range(hh):
        both_wait_send(*sib_out(h))
        q_out(1, o, h).wait_send()

        @pl.when(jnp.logical_not(first))
        def _():
            for half in range(2):
                q_out(0, half, h).wait_send()

        @pl.when(jnp.logical_not(last))
        def _():
            for half in range(2):
                q_out(2, half, h).wait_send()

    def drain(i, carry):
        b, sc, h = i // units, (i // hh) % 2, i % hh

        @pl.when(b != z)
        def _():
            flow_out(b, sc, h, z, 0)[0](both_wait_send)

            @pl.when(jnp.where(b < z, jnp.logical_not(last), jnp.logical_not(first)))
            def _():
                q_hop(b, sc, h, z).wait_send()

        return carry

    lax.fori_loop(0, n * units, drain, 0)


def per_device_paired(
    n,
    queries,
    new_keys,
    step_new_values,
    context_keys,
    context_values,
    cluster_centroid_keys,
    cluster_mean_values,
    cluster_page_slot,
    picks,
):
    num_steps, rows, num_heads, head_width = queries.shape
    kv_local, tokens = context_keys.shape[:2]
    cl = cluster_centroid_keys.shape[1]
    ncl = cluster_page_slot.shape[1]
    page = tokens // cl
    group = num_heads // kv_local
    hh = kv_local // 2
    nq = num_steps * rows * group
    bf16, f32, i16 = jnp.bfloat16, jnp.float32, jnp.int16
    q = queries.reshape(num_steps, rows, kv_local, group, head_width)
    q = q.transpose(2, 0, 1, 3, 4).reshape(2, hh, nq, head_width)
    ids = jnp.arange(ncl, dtype=jnp.int32)
    used = jnp.any(picks[..., None] == ids, axis=2)
    slots = jnp.any(
        jnp.logical_and(used[..., None], cluster_page_slot[None, :, :, None] == ids), axis=2
    )
    flags = jnp.concatenate([slots, jnp.logical_not(used)], axis=-1).astype(bf16)
    mask_groups = -(-2 * ncl // 128)
    flags = jnp.pad(flags.transpose(1, 0, 2), ((0, 0), (0, 16 - rows), (0, mask_groups * 128 - 2 * ncl)))
    flags = flags.reshape(kv_local, 16, mask_groups, 128).transpose(0, 2, 1, 3)
    flags = flags.reshape(2, hh, mask_groups * 16, 128)
    qx = jnp.concatenate([q, flags], axis=2)
    pad = ((0, 0), (0, 16 - cl), (0, 0))
    kx = jnp.concatenate([context_keys, jnp.pad(cluster_centroid_keys, pad)], axis=1)
    kx = kx.reshape(2, hh, tokens + 16, head_width)
    pad = ((0, 0), (0, 128 - cl), (0, 0))
    vx = jnp.concatenate([context_values, jnp.pad(cluster_mean_values, pad)], axis=1)
    vx = vx.transpose(0, 2, 1).reshape(2, hh, head_width, tokens + 128)
    nk = new_keys.transpose(2, 0, 1, 3).reshape(kv_local, num_steps * rows, head_width)
    nv = step_new_values.transpose(2, 0, 1, 3).reshape(kv_local, num_steps * rows, head_width)
    dims = (num_steps, rows, group, hh, cl, page, head_width, mask_groups)
    dma = pltpu.SemaphoreType.DMA
    vm = pltpu.VMEM
    unit = (n, 2, hh)
    out = pl.pallas_call(
        functools.partial(chain_kernel, n, dims),
        out_shape=jax.ShapeDtypeStruct((kv_local, nq, head_width), bf16),
        in_specs=[pl.BlockSpec(memory_space=pltpu.VMEM)] * 5,
        out_specs=pl.BlockSpec(memory_space=pltpu.VMEM),
        scratch_shapes=[
            vm(unit + qx.shape[2:], bf16),
            vm(kx.shape, bf16),
            vm(vx.shape, bf16),
            vm(unit + (head_width, nq), f32),
            vm(unit + (4, nq), f32),
            vm(unit + (head_width, nq), i16),
            vm(unit + (4, nq), f32),
            vm(unit + (head_width, nq), i16),
            vm(unit + (4, nq), f32),
            vm((2, 2, hh, head_width, nq), i16),
            vm((2, 2, hh, 4, nq), f32),
            vm((hh, head_width, nq), f32),
            vm((hh, 4, nq), f32),
            vm((kv_local, head_width, nq), f32),
            vm((kv_local, 4, nq), f32),
            vm((head_width, nq), f32),
            vm((4, nq), f32),
            vm((2, tokens + 128, nq), bf16),
            vm((2, tokens + 16, nq), f32),
            dma((3, 2, hh)),
            dma(unit),
            dma(unit),
            dma((2,) + unit),
            dma((2,) + unit),
            dma((2, 2, 2, hh)),
            dma((2, hh)),
            dma((2, hh)),
            dma((2,)),
            dma((2,)),
        ],
        compiler_params=pltpu.CompilerParams(
            collective_id=0, has_side_effects=True, vmem_limit_bytes=40 * 1024 * 1024
        ),
        cost_estimate=pl.CostEstimate(
            flops=8 * n * 2 * kv_local * nq * tokens * head_width,
            bytes_accessed=8 * 1024 * 1024,
            transcendentals=2 * n * kv_local * nq * tokens,
        ),
    )(qx, kx, vx, nk, nv)
    out = out.reshape(kv_local, num_steps, rows, group, head_width)
    return out.transpose(1, 2, 0, 3, 4).reshape(num_steps, rows, num_heads, head_width)


def solution(mesh):
    sizes = mesh.shape
    paired = sizes["row"] == 1 and sizes["ctx"] % 2 == 0 and sizes["ctx"] > 2
    step = functools.partial(per_device_paired, sizes["ctx"] // 2) if paired else per_device_plain
    return jax.shard_map(
        step,
        mesh=mesh,
        in_specs=(
            P(None, ("groups", "ctx", "row"), "rep", None),
            P(None, ("groups", "ctx", "row"), "rep", None),
            P(None, ("groups", "ctx", "row"), "rep", None),
            P("rep", ("groups", "ctx"), None),
            P("rep", ("groups", "ctx"), None),
            P("rep", ("groups", "ctx"), None),
            P("rep", ("groups", "ctx"), None),
            P("rep", "groups"),
            P(("groups", "ctx", "row"), "rep", None),
        ),
        out_specs=P(None, ("groups", "ctx", "row"), "rep", None),
        check_vma=False,
    )
```

```python
import functools
import math

import jax
import jax.numpy as jnp
from jax import lax
from jax.experimental import pallas as pl
from jax.experimental.pallas import tpu as pltpu
from jax.sharding import PartitionSpec as P

FLOOR_SCORE = -10000.0


def tail_block(queries, new_keys, step_new_values, logit_multiplier):
    num_steps, num_rows, num_heads, head_width = queries.shape
    kv_heads = new_keys.shape[2]
    grouped = queries.astype(jnp.float32).reshape(
        num_steps, num_rows, kv_heads, num_heads // kv_heads, head_width
    )
    scores = (
        jnp.einsum("srhgd,trhd->srhgt", grouped, new_keys.astype(jnp.float32)) * logit_multiplier
    )
    step_ids = jnp.arange(num_steps, dtype=jnp.int32)
    causal = (step_ids[None, :] <= step_ids[:, None])[:, None, None, None, :]
    block_top = jnp.max(jnp.where(causal, scores, FLOOR_SCORE), axis=-1)
    weights = jnp.where(causal, jnp.exp(scores - block_top[..., None]), 0.0)
    sum_total = jnp.sum(weights, axis=-1)
    rounded = weights.astype(jnp.bfloat16).astype(jnp.float32)
    tail_out = jnp.einsum("srhgt,trhd->srhgd", rounded, step_new_values.astype(jnp.float32))
    return (
        tail_out.reshape(num_steps, num_rows, num_heads, head_width),
        sum_total.reshape(num_steps, num_rows, num_heads),
        block_top.reshape(num_steps, num_rows, num_heads),
    )


def per_device_plain(
    queries,
    new_keys,
    step_new_values,
    context_keys,
    context_values,
    cluster_centroid_keys,
    cluster_mean_values,
    cluster_page_slot,
    picks,
):
    num_steps = queries.shape[0]
    num_heads = queries.shape[2]
    head_width = queries.shape[3]
    kv_local = context_keys.shape[0]
    span_tokens = context_keys.shape[1]
    cl_local = cluster_centroid_keys.shape[1]
    grouping_member_entries = span_tokens // cl_local
    query_group_size = num_heads // kv_local
    logit_multiplier = 1.0 / math.sqrt(head_width)
    membership_log_weight = math.log(grouping_member_entries)
    shard_index = lax.axis_index("ctx")
    gathered = lax.all_gather(queries, "ctx", axis=1, tiled=True)
    chosen = lax.all_gather(picks, "ctx", axis=0, tiled=True)
    rows_all = gathered.shape[1]
    cluster_ids = jnp.arange(cluster_page_slot.shape[1], dtype=jnp.int32)
    pick_hits = chosen[..., None] == cluster_ids
    picked_slots = jnp.sum(jnp.where(pick_hits, cluster_page_slot[None, :, None, :], 0), axis=-1)
    local_ids = shard_index * cl_local + jnp.arange(cl_local, dtype=jnp.int32)
    slot_used = jnp.any(picked_slots[..., None] == local_ids, axis=2)
    cluster_used = jnp.any(chosen[..., None] == local_ids, axis=2)
    step_outs, step_totals, step_tops = ([], [], [])
    for step_index in range(num_steps):
        head_outs, head_totals, head_tops = ([], [], [])
        for current_head_index in range(kv_local):
            generation_probe_vectors = gathered[
                step_index,
                :,
                current_head_index * query_group_size : (current_head_index + 1) * query_group_size,
                :,
            ].reshape(rows_all * query_group_size, head_width)
            exact_mask = slot_used[:, current_head_index][:, None, :, None]
            coarse_mask = jnp.logical_not(cluster_used[:, current_head_index])[:, None, :]
            exact_scores = (
                jnp.einsum(
                    "qd,kd->qk",
                    generation_probe_vectors,
                    context_keys[current_head_index],
                    preferred_element_type=jnp.float32,
                )
                * logit_multiplier
            )
            exact_scores = exact_scores.reshape(
                rows_all, query_group_size, cl_local, grouping_member_entries
            )
            prototype_logits = (
                jnp.einsum(
                    "qd,kd->qk",
                    generation_probe_vectors,
                    cluster_centroid_keys[current_head_index],
                    preferred_element_type=jnp.float32,
                )
                * logit_multiplier
                + membership_log_weight
            )
            prototype_logits = prototype_logits.reshape(rows_all, query_group_size, cl_local)
            block_top = jnp.maximum(
                jnp.max(jnp.where(exact_mask, exact_scores, FLOOR_SCORE), axis=(2, 3)),
                jnp.max(jnp.where(coarse_mask, prototype_logits, FLOOR_SCORE), axis=2),
            )
            exact_weights = jnp.where(
                exact_mask, jnp.exp(exact_scores - block_top[:, :, None, None]), 0.0
            )
            coarse_weights = jnp.where(
                coarse_mask, jnp.exp(prototype_logits - block_top[:, :, None]), 0.0
            )
            sum_total = jnp.sum(exact_weights, axis=(2, 3)) + jnp.sum(coarse_weights, axis=2)
            block_out = jnp.dot(
                exact_weights.astype(jnp.bfloat16).reshape(
                    rows_all * query_group_size, span_tokens
                ),
                context_values[current_head_index],
                preferred_element_type=jnp.float32,
            )
            block_out = block_out + jnp.dot(
                coarse_weights.astype(jnp.bfloat16).reshape(rows_all * query_group_size, cl_local),
                cluster_mean_values[current_head_index],
                preferred_element_type=jnp.float32,
            )
            head_outs.append(block_out.reshape(rows_all, query_group_size, head_width))
            head_totals.append(sum_total)
            head_tops.append(block_top)
        step_outs.append(jnp.concatenate(head_outs, axis=1))
        step_totals.append(jnp.concatenate(head_totals, axis=1))
        step_tops.append(jnp.concatenate(head_tops, axis=1))
    partial_outs = jnp.stack(step_outs)
    partial_totals = jnp.stack(step_totals)
    partial_tops = jnp.stack(step_tops)
    got_tops, got_totals, got_outs = (
        lax.all_to_all(partial_tops[None], "ctx", split_axis=2, concat_axis=0, tiled=True),
        lax.all_to_all(partial_totals[None], "ctx", split_axis=2, concat_axis=0, tiled=True),
        lax.all_to_all(partial_outs[None], "ctx", split_axis=2, concat_axis=0, tiled=True),
    )
    best_top = jnp.max(got_tops, axis=0)
    factor = jnp.exp(got_tops - best_top)
    sum_total = jnp.sum(factor * got_totals, axis=0)
    merged = jnp.sum(factor[..., None] * got_outs, axis=0)
    tail_out, tail_total, tail_top = tail_block(
        queries, new_keys, step_new_values, logit_multiplier
    )
    overall = jnp.maximum(best_top, tail_top)
    context_factor = jnp.exp(best_top - overall)
    tail_factor = jnp.exp(tail_top - overall)
    numer = context_factor[..., None] * merged + tail_factor[..., None] * tail_out
    denom = context_factor * sum_total + tail_factor * tail_total
    return (numer / denom[..., None]).astype(jnp.bfloat16)


MESH = pl.DeviceIdType.MESH
LOG2E = math.log2(math.e)
NT = (((1,), (1,)), ((), ()))
TN = (((0,), (0,)), ((), ()))


def chain_kernel(
    n, dims,
    queries, keys, cents, vx, picks, slots, nk, nv, out,
    qx,
    qbuf, kb, vb, part, part_st, inc, inc_st, snd, snd_st, fin, fin_st, sib, sib_st,
    tail, tail_st, acc, acc_st, wbuf, score,
    q_send, f_send, q_recv, s_send, s_recv, f_recv, b_send, b_recv, kv_send, kv_recv, k_sem,
):
    num_steps, rows, group, hh, cl, page, head_width, ncl = dims
    nq = num_steps * rows * group
    units = 2 * hh
    me = lax.axis_index("ctx")
    z, c = me // 2, me % 2
    o = 1 - c
    first, last = z == 0, z == n - 1
    scale2 = LOG2E / math.sqrt(head_width)
    coarse2 = LOG2E * math.log(page)
    floor2 = FLOOR_SCORE * LOG2E
    tokens = cl * page
    num_picks = picks.shape[2]

    def copy(src, dst, send, recv, chip, core):
        return pltpu.make_async_remote_copy(
            src_ref=src, dst_ref=dst, send_sem=send, recv_sem=recv,
            device_id={"ctx": chip * 2 + core}, device_id_type=MESH,
        )

    barrier = pltpu.get_barrier_semaphore()
    pl.semaphore_signal(barrier, inc=1, device_id={"ctx": z * 2 + o}, device_id_type=MESH)

    @pl.when(jnp.logical_not(first))
    def _():
        for core in range(2):
            pl.semaphore_signal(barrier, inc=1, device_id={"ctx": (z - 1) * 2 + core}, device_id_type=MESH)

    @pl.when(jnp.logical_not(last))
    def _():
        for core in range(2):
            pl.semaphore_signal(barrier, inc=1, device_id={"ctx": (z + 1) * 2 + core}, device_id_type=MESH)

    own_keys = pltpu.make_async_copy(keys.at[pl.ds(c * hh, hh)], kb.at[c, :, 0:tokens, :], k_sem)
    own_keys.start()

    def iota(shape, axis):
        return lax.broadcasted_iota(jnp.int32, shape, axis)

    page_of = jnp.where(slots[...] == iota((2 * hh, 128, 128), 1), 1.0, 0.0).astype(jnp.bfloat16)
    lane = iota((16, 128), 1)
    for hd in range(2 * hh):
        ids = picks[hd] + ncl
        used = jnp.zeros((16, 128), jnp.float32)
        for k in range(num_picks):
            used = jnp.where(ids[:, k : k + 1] == lane, 1.0, used)
        pages = lax.dot_general(used.astype(jnp.bfloat16), page_of[hd], NT, preferred_element_type=jnp.float32)
        coarse = jnp.where(jnp.logical_and(lane >= ncl, lane < 2 * ncl), 1.0 - used, 0.0)
        qx[hd // hh, hd % hh, 0:nq, :] = queries[hd]
        qx[hd // hh, hd % hh, nq : nq + 16, :] = (pages + coarse).astype(jnp.bfloat16)

    pl.semaphore_wait(barrier, 5 - 2 * first.astype(jnp.int32) - 2 * last.astype(jnp.int32))

    def q_out(way, half, h):
        chip = (z - 1, z, z + 1)[way]
        return copy(qx.at[half, h], qbuf.at[z, c, h], q_send.at[way, half, h], q_recv.at[z, c, h], chip, half)

    def q_hop(b, sc, h, chip):
        ref = qbuf.at[b, sc, h]
        return copy(ref, ref, f_send.at[b, sc, h], q_recv.at[b, sc, h], chip, c)

    def kv_out():
        return (
            copy(
                keys.at[pl.ds(o * hh, hh)], kb.at[c, :, 0:tokens, :], kv_send.at[0], kv_recv.at[0], z, o
            ),
            copy(cents.at[o], kb.at[c, :, tokens : tokens + 16, :], kv_send.at[2], kv_recv.at[2], z, o),
            copy(vx.at[o], vb.at[c], kv_send.at[1], kv_recv.at[1], z, o),
        )

    for one in kv_out():
        one.start()

    for h in range(hh):
        q_out(1, o, h).start()

        @pl.when(jnp.logical_not(first))
        def _():
            for half in range(2):
                q_out(0, half, h).start()

        @pl.when(jnp.logical_not(last))
        def _():
            for half in range(2):
                q_out(2, half, h).start()

    kb[c, :, tokens : tokens + 16, :] = cents[c]
    vb[c] = vx[c]
    qbuf[z, c] = qx[c]
    wbuf[...] = jnp.zeros_like(wbuf)

    def tail_head(hd, carry):
        q = qx[hd // hh, hd % hh, 0:nq, :]
        s = lax.dot_general(nk[hd], q, NT, preferred_element_type=jnp.float32) * scale2
        shape = (num_steps * rows, nq)
        t, r = iota(shape, 0) // rows, iota(shape, 0) % rows
        lane = iota(shape, 1)
        seen = jnp.logical_and((lane // group) % rows == r, t <= lane // (rows * group))
        s = jnp.where(seen, s, floor2)
        top = jnp.max(s, axis=0, keepdims=True)
        w = jnp.where(seen, jnp.exp2(s - top), 0.0)
        tail_st[hd, 0:1, :] = top
        tail_st[hd, 1:2, :] = jnp.sum(w, axis=0, keepdims=True)
        tail[hd] = lax.dot_general(nv[hd], w.astype(jnp.bfloat16), TN, preferred_element_type=jnp.float32)
        return carry

    lax.fori_loop(0, 2 * hh, tail_head, 0)

    sel_rows = 48
    si, sl = iota((sel_rows, 128), 0), iota((sel_rows, 128), 1)
    in_page = si < 2 * cl
    blk = jnp.where(si >= 32, 1, 0)
    j = si - 16 - 16 * blk
    in_coarse = jnp.logical_and(si >= 16, j < cl)
    target = jnp.where(in_page, z * 2 * cl + si, jnp.where(in_coarse, ncl + (z * 2 + blk) * cl + j, -1))
    select = jnp.where(sl == target, 1.0, 0.0).astype(jnp.bfloat16)
    spread = jnp.where((iota((16, nq), 1) // group) % rows == iota((16, nq), 0), 1.0, 0.0).astype(jnp.bfloat16)

    own_keys.wait()
    for one in kv_out():
        one.wait_recv()

    def compute(b, sc, h):
        q = qbuf[b, sc, h, 0:nq, :]
        bits = qbuf[b, sc, h, nq : nq + 16, :]
        flags = lax.dot_general(select, bits, NT, preferred_element_type=jnp.float32)
        flags = jnp.dot(flags.astype(jnp.bfloat16), spread, preferred_element_type=jnp.float32)
        outs = []
        for d in range(2):
            score[d] = lax.dot_general(kb[d, h], q, NT, preferred_element_type=jnp.float32) * scale2
        for d in range(2):
            coarse_on = flags[16 + 16 * d : 32 + 16 * d, :] > 0.5
            coarse = score[d, tokens : tokens + 16, :] + coarse2
            top = jnp.max(jnp.where(coarse_on, coarse, floor2), axis=0, keepdims=True)
            on = [flags[d * cl + p : d * cl + p + 1, :] > 0.5 for p in range(cl)]
            for p in range(cl):
                page_top = jnp.max(score[d, p * page : (p + 1) * page, :], axis=0, keepdims=True)
                top = jnp.maximum(top, jnp.where(on[p], page_top, floor2))
            wc = jnp.where(coarse_on, jnp.exp2(coarse - top), 0.0)
            wbuf[d, tokens : tokens + 16, :] = wc.astype(jnp.bfloat16)
            total = jnp.sum(wc, axis=0, keepdims=True)
            for p in range(cl):
                w = jnp.exp2(score[d, p * page : (p + 1) * page, :] - jnp.where(on[p], top, 1e30))
                wbuf[d, p * page : (p + 1) * page, :] = w.astype(jnp.bfloat16)
                total = total + jnp.sum(w, axis=0, keepdims=True)
            outs.append((jnp.dot(vb[d, h], wbuf[d], preferred_element_type=jnp.float32), total, top))
        (o0, l0, m0), (o1, l1, m1) = outs
        top = jnp.maximum(m0, m1)
        a0, a1 = jnp.exp2(m0 - top), jnp.exp2(m1 - top)
        part[b, sc, h] = a0 * o0 + a1 * o1
        part_st[b, sc, h, 0:1, :] = top
        part_st[b, sc, h, 1:2, :] = a0 * l0 + a1 * l1

    def merge(o_ref, st_ref, values, st):
        m0, m1 = st_ref[0:1, :], st[0:1, :]
        top = jnp.maximum(m0, m1)
        a0, a1 = jnp.exp2(m0 - top), jnp.exp2(m1 - top)
        o_ref[...] = a0 * o_ref[...] + a1 * values
        st_ref[1:2, :] = a0 * st_ref[1:2, :] + a1 * st[1:2, :]
        st_ref[0:1, :] = top

    def decode(ref, st_ref):
        return ref[...].astype(jnp.int32).astype(jnp.float32) * st_ref[2:3, :]

    def flow_out(b, sc, h, chip, way):
        def hop(fn):
            fn(
                copy(snd.at[b, sc, h], inc.at[b, sc, h], s_send.at[0, b, sc, h], s_recv.at[0, b, sc, h], chip, c),
                copy(snd_st.at[b, sc, h], inc_st.at[b, sc, h], s_send.at[1, b, sc, h], s_recv.at[1, b, sc, h], chip, c),
            )

        def home(fn):
            fn(
                copy(snd.at[b, sc, h], fin.at[way, c, h], s_send.at[0, b, sc, h], f_recv.at[0, way, c, h], b, sc),
                copy(snd_st.at[b, sc, h], fin_st.at[way, c, h], s_send.at[1, b, sc, h], f_recv.at[1, way, c, h], b, sc),
            )

        return hop, home

    def both_start(x, y):
        x.start()
        y.start()

    def both_wait_send(x, y):
        x.wait_send()
        y.wait_send()

    def both_wait_recv(x, y):
        x.wait_recv()
        y.wait_recv()

    def sib_out(h):
        return (
            copy(part.at[z, o, h], sib.at[h], b_send.at[0, h], b_recv.at[0, h], z, o),
            copy(part_st.at[z, o, h], sib_st.at[h], b_send.at[1, h], b_recv.at[1, h], z, o),
        )

    lead = units - 1
    late = jnp.maximum(z, n - 1 - z) + 1

    def slot(i):
        dist = i // (2 * units)
        u = (i // 2) % units
        side = i % 2
        return dist, side, (u // hh + c) % 2, u % hh, z + (2 * side - 1) * dist, u

    def step(i, carry):
        dist, side, sc, h, b, _ = slot(i + 2 * lead)

        @pl.when(jnp.logical_and(dist > 0, jnp.logical_and(b >= 0, b < n)))
        def _():
            bb = jnp.clip(b, 0, n - 1)
            q_hop(bb, sc, h, z).wait_recv()

            @pl.when(jnp.logical_and(bb < z, jnp.logical_not(last)))
            def _():
                q_hop(bb, sc, h, z + 1).start()

            @pl.when(jnp.logical_and(bb > z, jnp.logical_not(first)))
            def _():
                q_hop(bb, sc, h, z - 1).start()

        dist, side, sc, h, b, u = slot(i)
        own = jnp.logical_or(dist == 0, dist == late)
        b = jnp.where(own, z, b)
        valid = jnp.where(
            own,
            jnp.logical_and(side == 0, jnp.where(dist == 0, u < hh, u >= hh)),
            jnp.logical_and(b >= 0, b < n),
        )

        @pl.when(valid)
        def _():
            bb = jnp.clip(b, 0, n - 1)

            @pl.when(jnp.logical_and(bb == z, sc != c))
            def _():
                q_hop(bb, sc, h, z).wait_recv()

            compute(bb, sc, h)

            @pl.when(jnp.logical_and(bb == z, sc != c))
            def _():
                both_start(*sib_out(h))

        bm = jnp.where(side == 0, 2 * (n - 1) - z - dist, dist - z)
        flows = jnp.where(
            side == 0, jnp.logical_and(bm >= 0, bm < z), jnp.logical_and(bm > z, bm < n)
        )

        @pl.when(flows)
        def _():
            bb = jnp.clip(bm, 0, n - 1)
            o_ref, st_ref = part.at[bb, sc, h], part_st.at[bb, sc, h]

            @pl.when(jnp.where(side == 0, jnp.logical_not(last), jnp.logical_not(first)))
            def _():
                flow_out(bb, sc, h, z, side)[0](both_wait_recv)
                merge(o_ref, st_ref, decode(inc.at[bb, sc, h], inc_st.at[bb, sc, h]), inc_st.at[bb, sc, h])

            values = o_ref[...]
            size = jnp.max(jnp.abs(values), axis=0, keepdims=True)
            fit = 32767.0 / jnp.maximum(size, 1e-30)
            snd[bb, sc, h] = jnp.round(values * fit).astype(jnp.int32).astype(jnp.int16)
            snd_st[bb, sc, h, 0:2, :] = st_ref[0:2, :]
            snd_st[bb, sc, h, 2:3, :] = jnp.maximum(size, 1e-30) * (1.0 / 32767.0)
            chip = z + 2 * side - 1
            hop, home = flow_out(bb, sc, h, chip, side)

            @pl.when(chip == bb)
            def _():
                home(both_start)

            @pl.when(chip != bb)
            def _():
                hop(both_start)

        return carry

    lax.fori_loop(0, (2 * n - 1) * 2 * units, step, 0)

    def finish(i, carry):
        half = (i // hh + c) % 2
        h = i % hh
        hd = half * hh + h
        acc[...] = tail[hd]
        acc_st[...] = tail_st[hd]

        @pl.when(half == c)
        def _():
            merge(acc, acc_st, part[z, c, h], part_st.at[z, c, h])

        @pl.when(half != c)
        def _():
            both_wait_recv(*sib_out(h))
            merge(acc, acc_st, sib[h], sib_st.at[h])

        def arrive(way):
            both_wait_recv(
                copy(snd.at[0, 0, 0], fin.at[way, half, h], s_send.at[0, 0, 0, 0], f_recv.at[0, way, half, h], z, c),
                copy(snd_st.at[0, 0, 0], fin_st.at[way, half, h], s_send.at[1, 0, 0, 0], f_recv.at[1, way, half, h], z, c),
            )
            merge(acc, acc_st, decode(fin.at[way, half, h], fin_st.at[way, half, h]), fin_st.at[way, half, h])

        @pl.when(jnp.logical_not(last))
        def _():
            arrive(0)

        @pl.when(jnp.logical_not(first))
        def _():
            arrive(1)

        out[hd] = jnp.transpose(acc[...] / acc_st[1:2, :]).astype(jnp.bfloat16)
        return carry

    lax.fori_loop(0, units, finish, 0)

    for one in kv_out():
        one.wait_send()
    for h in range(hh):
        both_wait_send(*sib_out(h))
        q_out(1, o, h).wait_send()

        @pl.when(jnp.logical_not(first))
        def _():
            for half in range(2):
                q_out(0, half, h).wait_send()

        @pl.when(jnp.logical_not(last))
        def _():
            for half in range(2):
                q_out(2, half, h).wait_send()

    def drain(i, carry):
        b, sc, h = i // units, (i // hh) % 2, i % hh

        @pl.when(b != z)
        def _():
            flow_out(b, sc, h, z, 0)[0](both_wait_send)

            @pl.when(jnp.where(b < z, jnp.logical_not(last), jnp.logical_not(first)))
            def _():
                q_hop(b, sc, h, z).wait_send()

        return carry

    lax.fori_loop(0, n * units, drain, 0)


def per_device_paired(
    n,
    queries,
    new_keys,
    step_new_values,
    context_keys,
    context_values,
    cluster_centroid_keys,
    cluster_mean_values,
    cluster_page_slot,
    picks,
):
    num_steps, rows, num_heads, head_width = queries.shape
    kv_local, tokens = context_keys.shape[:2]
    cl = cluster_centroid_keys.shape[1]
    ncl = cluster_page_slot.shape[1]
    if 2 * ncl > 128 or rows > 16 or 2 * cl > 16 or kv_local % 2:
        return per_device_plain(
            queries, new_keys, step_new_values, context_keys, context_values,
            cluster_centroid_keys, cluster_mean_values, cluster_page_slot, picks,
        )
    page = tokens // cl
    group = num_heads // kv_local
    hh = kv_local // 2
    nq = num_steps * rows * group
    bf16, f32, i16 = jnp.bfloat16, jnp.float32, jnp.int16
    q = queries.reshape(num_steps, rows, kv_local, group, head_width)
    q = q.transpose(2, 0, 1, 3, 4).reshape(kv_local, nq, head_width)
    chosen = jnp.pad(picks.transpose(1, 0, 2), ((0, 0), (0, 16 - rows), (0, 0)), constant_values=-1)
    slots = jnp.pad(cluster_page_slot, ((0, 0), (ncl, 128 - 2 * ncl)), constant_values=-1)[:, None, :]
    pad = ((0, 0), (0, 16 - cl), (0, 0))
    cents = jnp.pad(cluster_centroid_keys, pad).reshape(2, hh, 16, head_width)
    pad = ((0, 0), (0, 128 - cl), (0, 0))
    vx = jnp.concatenate([context_values, jnp.pad(cluster_mean_values, pad)], axis=1)
    vx = vx.transpose(0, 2, 1).reshape(2, hh, head_width, tokens + 128)
    nk = new_keys.transpose(2, 0, 1, 3).reshape(kv_local, num_steps * rows, head_width)
    nv = step_new_values.transpose(2, 0, 1, 3).reshape(kv_local, num_steps * rows, head_width)
    dims = (num_steps, rows, group, hh, cl, page, head_width, ncl)
    dma = pltpu.SemaphoreType.DMA
    vm = pltpu.VMEM
    unit = (n, 2, hh)
    out = pl.pallas_call(
        functools.partial(chain_kernel, n, dims),
        out_shape=jax.ShapeDtypeStruct((kv_local, nq, head_width), bf16),
        in_specs=[pl.BlockSpec(memory_space=pl.ANY if i == 1 else pltpu.VMEM) for i in range(8)],
        out_specs=pl.BlockSpec(memory_space=pltpu.VMEM),
        scratch_shapes=[
            vm((2, hh, nq + 16, head_width), bf16),
            vm(unit + (nq + 16, head_width), bf16),
            vm((2, hh, tokens + 16, head_width), bf16),
            vm(vx.shape, bf16),
            vm(unit + (head_width, nq), f32),
            vm(unit + (4, nq), f32),
            vm(unit + (head_width, nq), i16),
            vm(unit + (4, nq), f32),
            vm(unit + (head_width, nq), i16),
            vm(unit + (4, nq), f32),
            vm((2, 2, hh, head_width, nq), i16),
            vm((2, 2, hh, 4, nq), f32),
            vm((hh, head_width, nq), f32),
            vm((hh, 4, nq), f32),
            vm((kv_local, head_width, nq), f32),
            vm((kv_local, 4, nq), f32),
            vm((head_width, nq), f32),
            vm((4, nq), f32),
            vm((2, tokens + 128, nq), bf16),
            vm((2, tokens + 16, nq), f32),
            dma((3, 2, hh)),
            dma(unit),
            dma(unit),
            dma((2,) + unit),
            dma((2,) + unit),
            dma((2, 2, 2, hh)),
            dma((2, hh)),
            dma((2, hh)),
            dma((3,)),
            dma((3,)),
            dma,
        ],
        compiler_params=pltpu.CompilerParams(
            collective_id=0, has_side_effects=True, vmem_limit_bytes=40 * 1024 * 1024
        ),
        cost_estimate=pl.CostEstimate(
            flops=8 * n * 2 * kv_local * nq * tokens * head_width,
            bytes_accessed=8 * 1024 * 1024,
            transcendentals=2 * n * kv_local * nq * tokens,
        ),
    )(q, context_keys, cents, vx, chosen, slots, nk, nv)
    out = out.reshape(kv_local, num_steps, rows, group, head_width)
    return out.transpose(1, 2, 0, 3, 4).reshape(num_steps, rows, num_heads, head_width)


def solution(mesh):
    sizes = mesh.shape
    paired = sizes["row"] == 1 and sizes["ctx"] % 2 == 0 and sizes["ctx"] > 2
    step = functools.partial(per_device_paired, sizes["ctx"] // 2) if paired else per_device_plain
    return jax.shard_map(
        step,
        mesh=mesh,
        in_specs=(
            P(None, ("groups", "ctx", "row"), "rep", None),
            P(None, ("groups", "ctx", "row"), "rep", None),
            P(None, ("groups", "ctx", "row"), "rep", None),
            P("rep", ("groups", "ctx"), None),
            P("rep", ("groups", "ctx"), None),
            P("rep", ("groups", "ctx"), None),
            P("rep", ("groups", "ctx"), None),
            P("rep", "groups"),
            P(("groups", "ctx", "row"), "rep", None),
        ),
        out_specs=P(None, ("groups", "ctx", "row"), "rep", None),
        check_vma=False,
    )
```

```python
import functools
import math

import jax
import jax.numpy as jnp
from jax import lax
from jax.experimental import pallas as pl
from jax.experimental.pallas import tpu as pltpu
from jax.sharding import PartitionSpec as P

FLOOR_SCORE = -10000.0


def tail_block(queries, new_keys, step_new_values, logit_multiplier):
    num_steps, num_rows, num_heads, head_width = queries.shape
    kv_heads = new_keys.shape[2]
    grouped = queries.astype(jnp.float32).reshape(
        num_steps, num_rows, kv_heads, num_heads // kv_heads, head_width
    )
    scores = (
        jnp.einsum("srhgd,trhd->srhgt", grouped, new_keys.astype(jnp.float32)) * logit_multiplier
    )
    step_ids = jnp.arange(num_steps, dtype=jnp.int32)
    causal = (step_ids[None, :] <= step_ids[:, None])[:, None, None, None, :]
    block_top = jnp.max(jnp.where(causal, scores, FLOOR_SCORE), axis=-1)
    weights = jnp.where(causal, jnp.exp(scores - block_top[..., None]), 0.0)
    sum_total = jnp.sum(weights, axis=-1)
    rounded = weights.astype(jnp.bfloat16).astype(jnp.float32)
    tail_out = jnp.einsum("srhgt,trhd->srhgd", rounded, step_new_values.astype(jnp.float32))
    return (
        tail_out.reshape(num_steps, num_rows, num_heads, head_width),
        sum_total.reshape(num_steps, num_rows, num_heads),
        block_top.reshape(num_steps, num_rows, num_heads),
    )


def per_device_plain(
    queries,
    new_keys,
    step_new_values,
    context_keys,
    context_values,
    cluster_centroid_keys,
    cluster_mean_values,
    cluster_page_slot,
    picks,
):
    num_steps = queries.shape[0]
    num_heads = queries.shape[2]
    head_width = queries.shape[3]
    kv_local = context_keys.shape[0]
    span_tokens = context_keys.shape[1]
    cl_local = cluster_centroid_keys.shape[1]
    grouping_member_entries = span_tokens // cl_local
    query_group_size = num_heads // kv_local
    logit_multiplier = 1.0 / math.sqrt(head_width)
    membership_log_weight = math.log(grouping_member_entries)
    shard_index = lax.axis_index("ctx")
    gathered = lax.all_gather(queries, "ctx", axis=1, tiled=True)
    chosen = lax.all_gather(picks, "ctx", axis=0, tiled=True)
    rows_all = gathered.shape[1]
    cluster_ids = jnp.arange(cluster_page_slot.shape[1], dtype=jnp.int32)
    pick_hits = chosen[..., None] == cluster_ids
    picked_slots = jnp.sum(jnp.where(pick_hits, cluster_page_slot[None, :, None, :], 0), axis=-1)
    local_ids = shard_index * cl_local + jnp.arange(cl_local, dtype=jnp.int32)
    slot_used = jnp.any(picked_slots[..., None] == local_ids, axis=2)
    cluster_used = jnp.any(chosen[..., None] == local_ids, axis=2)
    step_outs, step_totals, step_tops = ([], [], [])
    for step_index in range(num_steps):
        head_outs, head_totals, head_tops = ([], [], [])
        for current_head_index in range(kv_local):
            generation_probe_vectors = gathered[
                step_index,
                :,
                current_head_index * query_group_size : (current_head_index + 1) * query_group_size,
                :,
            ].reshape(rows_all * query_group_size, head_width)
            exact_mask = slot_used[:, current_head_index][:, None, :, None]
            coarse_mask = jnp.logical_not(cluster_used[:, current_head_index])[:, None, :]
            exact_scores = (
                jnp.einsum(
                    "qd,kd->qk",
                    generation_probe_vectors,
                    context_keys[current_head_index],
                    preferred_element_type=jnp.float32,
                )
                * logit_multiplier
            )
            exact_scores = exact_scores.reshape(
                rows_all, query_group_size, cl_local, grouping_member_entries
            )
            prototype_logits = (
                jnp.einsum(
                    "qd,kd->qk",
                    generation_probe_vectors,
                    cluster_centroid_keys[current_head_index],
                    preferred_element_type=jnp.float32,
                )
                * logit_multiplier
                + membership_log_weight
            )
            prototype_logits = prototype_logits.reshape(rows_all, query_group_size, cl_local)
            block_top = jnp.maximum(
                jnp.max(jnp.where(exact_mask, exact_scores, FLOOR_SCORE), axis=(2, 3)),
                jnp.max(jnp.where(coarse_mask, prototype_logits, FLOOR_SCORE), axis=2),
            )
            exact_weights = jnp.where(
                exact_mask, jnp.exp(exact_scores - block_top[:, :, None, None]), 0.0
            )
            coarse_weights = jnp.where(
                coarse_mask, jnp.exp(prototype_logits - block_top[:, :, None]), 0.0
            )
            sum_total = jnp.sum(exact_weights, axis=(2, 3)) + jnp.sum(coarse_weights, axis=2)
            block_out = jnp.dot(
                exact_weights.astype(jnp.bfloat16).reshape(
                    rows_all * query_group_size, span_tokens
                ),
                context_values[current_head_index],
                preferred_element_type=jnp.float32,
            )
            block_out = block_out + jnp.dot(
                coarse_weights.astype(jnp.bfloat16).reshape(rows_all * query_group_size, cl_local),
                cluster_mean_values[current_head_index],
                preferred_element_type=jnp.float32,
            )
            head_outs.append(block_out.reshape(rows_all, query_group_size, head_width))
            head_totals.append(sum_total)
            head_tops.append(block_top)
        step_outs.append(jnp.concatenate(head_outs, axis=1))
        step_totals.append(jnp.concatenate(head_totals, axis=1))
        step_tops.append(jnp.concatenate(head_tops, axis=1))
    partial_outs = jnp.stack(step_outs)
    partial_totals = jnp.stack(step_totals)
    partial_tops = jnp.stack(step_tops)
    got_tops, got_totals, got_outs = (
        lax.all_to_all(partial_tops[None], "ctx", split_axis=2, concat_axis=0, tiled=True),
        lax.all_to_all(partial_totals[None], "ctx", split_axis=2, concat_axis=0, tiled=True),
        lax.all_to_all(partial_outs[None], "ctx", split_axis=2, concat_axis=0, tiled=True),
    )
    best_top = jnp.max(got_tops, axis=0)
    factor = jnp.exp(got_tops - best_top)
    sum_total = jnp.sum(factor * got_totals, axis=0)
    merged = jnp.sum(factor[..., None] * got_outs, axis=0)
    tail_out, tail_total, tail_top = tail_block(
        queries, new_keys, step_new_values, logit_multiplier
    )
    overall = jnp.maximum(best_top, tail_top)
    context_factor = jnp.exp(best_top - overall)
    tail_factor = jnp.exp(tail_top - overall)
    numer = context_factor[..., None] * merged + tail_factor[..., None] * tail_out
    denom = context_factor * sum_total + tail_factor * tail_total
    return (numer / denom[..., None]).astype(jnp.bfloat16)


MESH = pl.DeviceIdType.MESH
LOG2E = math.log2(math.e)
NT = (((1,), (1,)), ((), ()))
TN = (((0,), (0,)), ((), ()))


def chain_kernel(
    n, dims,
    queries, keys, cents, vx, picks, slots, nk, nv, out,
    qx,
    qbuf, kb, vb, part, part_st, inc, inc_st, snd, snd_st, fin, fin_st, sib, sib_st,
    tail, tail_st, acc, acc_st, wbuf, score,
    q_send, f_send, q_recv, s_send, s_recv, f_recv, b_send, b_recv, kv_send, kv_recv, k_sem,
):
    num_steps, rows, group, hh, cl, page, head_width, ncl = dims
    nq = num_steps * rows * group
    units = 2 * hh
    me = lax.axis_index("ctx")
    z, c = me // 2, me % 2
    o = 1 - c
    first, last = z == 0, z == n - 1
    scale2 = LOG2E / math.sqrt(head_width)
    coarse2 = LOG2E * math.log(page)
    floor2 = FLOOR_SCORE * LOG2E
    tokens = cl * page
    num_picks = picks.shape[2]

    def copy(src, dst, send, recv, chip, core):
        return pltpu.make_async_remote_copy(
            src_ref=src, dst_ref=dst, send_sem=send, recv_sem=recv,
            device_id={"ctx": chip * 2 + core}, device_id_type=MESH,
        )

    barrier = pltpu.get_barrier_semaphore()
    pl.semaphore_signal(barrier, inc=1, device_id={"ctx": z * 2 + o}, device_id_type=MESH)

    @pl.when(jnp.logical_not(first))
    def _():
        for core in range(2):
            pl.semaphore_signal(barrier, inc=1, device_id={"ctx": (z - 1) * 2 + core}, device_id_type=MESH)

    @pl.when(jnp.logical_not(last))
    def _():
        for core in range(2):
            pl.semaphore_signal(barrier, inc=1, device_id={"ctx": (z + 1) * 2 + core}, device_id_type=MESH)

    own_keys = pltpu.make_async_copy(keys.at[pl.ds(c * hh, hh)], kb.at[c, :, 0:tokens, :], k_sem)
    own_keys.start()

    def iota(shape, axis):
        return lax.broadcasted_iota(jnp.int32, shape, axis)

    page_of = jnp.where(slots[...] == iota((2 * hh, 128, 128), 1), 1.0, 0.0).astype(jnp.bfloat16)
    lane = iota((16, 128), 1)
    for hd in range(2 * hh):
        ids = picks[hd] + ncl
        used = jnp.zeros((16, 128), jnp.float32)
        for k in range(num_picks):
            used = jnp.where(ids[:, k : k + 1] == lane, 1.0, used)
        pages = lax.dot_general(used.astype(jnp.bfloat16), page_of[hd], NT, preferred_element_type=jnp.float32)
        coarse = jnp.where(jnp.logical_and(lane >= ncl, lane < 2 * ncl), 1.0 - used, 0.0)
        qx[hd // hh, hd % hh, 0:nq, :] = queries[hd]
        qx[hd // hh, hd % hh, nq : nq + 16, :] = (pages + coarse).astype(jnp.bfloat16)

    pl.semaphore_wait(barrier, 5 - 2 * first.astype(jnp.int32) - 2 * last.astype(jnp.int32))

    def q_out(way, half, h):
        chip = (z - 1, z, z + 1)[way]
        return copy(qx.at[half, h], qbuf.at[z, c, h], q_send.at[way, half, h], q_recv.at[z, c, h], chip, half)

    def q_hop(b, sc, h, chip):
        ref = qbuf.at[b, sc, h]
        return copy(ref, ref, f_send.at[b, sc, h], q_recv.at[b, sc, h], chip, c)

    def kv_out():
        return (
            copy(
                keys.at[pl.ds(o * hh, hh)], kb.at[c, :, 0:tokens, :], kv_send.at[0], kv_recv.at[0], z, o
            ),
            copy(cents.at[o], kb.at[c, :, tokens : tokens + 16, :], kv_send.at[2], kv_recv.at[2], z, o),
            copy(vx.at[o], vb.at[c], kv_send.at[1], kv_recv.at[1], z, o),
        )

    for h in range(hh // 2):

        @pl.when(jnp.logical_not(first))
        def _():
            for half in range(2):
                q_out(0, half, h).start()

        @pl.when(jnp.logical_not(last))
        def _():
            for half in range(2):
                q_out(2, half, h).start()

    for one in kv_out():
        one.start()

    for h in range(hh):
        q_out(1, o, h).start()

    kb[c, :, tokens : tokens + 16, :] = cents[c]
    vb[c] = vx[c]
    qbuf[z, c] = qx[c]
    wbuf[...] = jnp.zeros_like(wbuf)

    def tail_head(hd, carry):
        q = qx[hd // hh, hd % hh, 0:nq, :]
        s = lax.dot_general(nk[hd], q, NT, preferred_element_type=jnp.float32) * scale2
        shape = (num_steps * rows, nq)
        t, r = iota(shape, 0) // rows, iota(shape, 0) % rows
        lane = iota(shape, 1)
        seen = jnp.logical_and((lane // group) % rows == r, t <= lane // (rows * group))
        s = jnp.where(seen, s, floor2)
        top = jnp.max(s, axis=0, keepdims=True)
        w = jnp.where(seen, jnp.exp2(s - top), 0.0)
        tail_st[hd, 0:1, :] = top
        tail_st[hd, 1:2, :] = jnp.sum(w, axis=0, keepdims=True)
        tail[hd] = lax.dot_general(nv[hd], w.astype(jnp.bfloat16), TN, preferred_element_type=jnp.float32)
        return carry

    lax.fori_loop(0, 2 * hh, tail_head, 0)

    sel_rows = 48
    si, sl = iota((sel_rows, 128), 0), iota((sel_rows, 128), 1)
    in_page = si < 2 * cl
    blk = jnp.where(si >= 32, 1, 0)
    j = si - 16 - 16 * blk
    in_coarse = jnp.logical_and(si >= 16, j < cl)
    target = jnp.where(in_page, z * 2 * cl + si, jnp.where(in_coarse, ncl + (z * 2 + blk) * cl + j, -1))
    select = jnp.where(sl == target, 1.0, 0.0).astype(jnp.bfloat16)
    spread = jnp.where((iota((16, nq), 1) // group) % rows == iota((16, nq), 0), 1.0, 0.0).astype(jnp.bfloat16)

    own_keys.wait()
    for one in kv_out():
        one.wait_recv()

    def compute(b, sc, h):
        q = qbuf[b, sc, h, 0:nq, :]
        bits = qbuf[b, sc, h, nq : nq + 16, :]
        flags = lax.dot_general(select, bits, NT, preferred_element_type=jnp.float32)
        flags = jnp.dot(flags.astype(jnp.bfloat16), spread, preferred_element_type=jnp.float32)
        outs = []
        for d in range(2):
            score[d] = lax.dot_general(kb[d, h], q, NT, preferred_element_type=jnp.float32) * scale2
        for d in range(2):
            coarse_on = flags[16 + 16 * d : 32 + 16 * d, :] > 0.5
            coarse = score[d, tokens : tokens + 16, :] + coarse2
            top = jnp.max(jnp.where(coarse_on, coarse, floor2), axis=0, keepdims=True)
            on = [flags[d * cl + p : d * cl + p + 1, :] > 0.5 for p in range(cl)]
            for p in range(cl):
                page_top = jnp.max(score[d, p * page : (p + 1) * page, :], axis=0, keepdims=True)
                top = jnp.maximum(top, jnp.where(on[p], page_top, floor2))
            wc = jnp.where(coarse_on, jnp.exp2(coarse - top), 0.0)
            wbuf[d, tokens : tokens + 16, :] = wc.astype(jnp.bfloat16)
            total = jnp.sum(wc, axis=0, keepdims=True)
            for p in range(cl):
                w = jnp.exp2(score[d, p * page : (p + 1) * page, :] - jnp.where(on[p], top, 1e30))
                wbuf[d, p * page : (p + 1) * page, :] = w.astype(jnp.bfloat16)
                total = total + jnp.sum(w, axis=0, keepdims=True)
            outs.append((jnp.dot(vb[d, h], wbuf[d], preferred_element_type=jnp.float32), total, top))
        (o0, l0, m0), (o1, l1, m1) = outs
        top = jnp.maximum(m0, m1)
        a0, a1 = jnp.exp2(m0 - top), jnp.exp2(m1 - top)
        part[b, sc, h] = a0 * o0 + a1 * o1
        part_st[b, sc, h, 0:1, :] = top
        part_st[b, sc, h, 1:2, :] = a0 * l0 + a1 * l1

    def merge(o_ref, st_ref, values, st):
        m0, m1 = st_ref[0:1, :], st[0:1, :]
        top = jnp.maximum(m0, m1)
        a0, a1 = jnp.exp2(m0 - top), jnp.exp2(m1 - top)
        o_ref[...] = a0 * o_ref[...] + a1 * values
        st_ref[1:2, :] = a0 * st_ref[1:2, :] + a1 * st[1:2, :]
        st_ref[0:1, :] = top

    def decode(ref, st_ref):
        return ref[...].astype(jnp.int32).astype(jnp.float32) * st_ref[2:3, :]

    def flow_out(b, sc, h, chip, way):
        def hop(fn):
            fn(
                copy(snd.at[b, sc, h], inc.at[b, sc, h], s_send.at[0, b, sc, h], s_recv.at[0, b, sc, h], chip, c),
                copy(snd_st.at[b, sc, h], inc_st.at[b, sc, h], s_send.at[1, b, sc, h], s_recv.at[1, b, sc, h], chip, c),
            )

        def home(fn):
            fn(
                copy(snd.at[b, sc, h], fin.at[way, c, h], s_send.at[0, b, sc, h], f_recv.at[0, way, c, h], b, sc),
                copy(snd_st.at[b, sc, h], fin_st.at[way, c, h], s_send.at[1, b, sc, h], f_recv.at[1, way, c, h], b, sc),
            )

        return hop, home

    def both_start(x, y):
        x.start()
        y.start()

    def both_wait_send(x, y):
        x.wait_send()
        y.wait_send()

    def both_wait_recv(x, y):
        x.wait_recv()
        y.wait_recv()

    def sib_out(h):
        return (
            copy(part.at[z, o, h], sib.at[h], b_send.at[0, h], b_recv.at[0, h], z, o),
            copy(part_st.at[z, o, h], sib_st.at[h], b_send.at[1, h], b_recv.at[1, h], z, o),
        )

    def subslot(i):
        k = i % units
        side = k % 2
        place = jnp.where(side == 0, z, n - 1 - z)
        return i // units - 1, side, (k // 2 + c) % 2, k // 4, place

    def event(t, side, place):
        wave = jnp.where(t < place, 0, 1)
        dist = jnp.where(t < place, t + 1, 2 * place - t)
        valid = jnp.logical_and(t >= 0, t < 2 * place)
        return wave, jnp.clip(z + (2 * side - 1) * dist, 0, n - 1), valid

    def flow(bs, wave, side, sc, hw, place):
        @pl.when(jnp.logical_and(bs >= 0, bs < place))
        def _():
            bb = jnp.clip(jnp.where(side == 0, bs, n - 1 - bs), 0, n - 1)
            h = wave * (hh // 2) + hw
            o_ref, st_ref = part.at[bb, sc, h], part_st.at[bb, sc, h]

            @pl.when(place < n - 1)
            def _():
                flow_out(bb, sc, h, z, side)[0](both_wait_recv)
                merge(o_ref, st_ref, decode(inc.at[bb, sc, h], inc_st.at[bb, sc, h]), inc_st.at[bb, sc, h])

            values = o_ref[...]
            size = jnp.maximum(jnp.max(jnp.abs(values), axis=0, keepdims=True), 1e-30)
            snd[bb, sc, h] = jnp.round(values * (32767.0 / size)).astype(jnp.int32).astype(jnp.int16)
            snd_st[bb, sc, h, 0:2, :] = st_ref[0:2, :]
            snd_st[bb, sc, h, 2:3, :] = size * (1.0 / 32767.0)
            chip = z + 2 * side - 1
            hop, home = flow_out(bb, sc, h, chip, side)

            @pl.when(chip == bb)
            def _():
                home(both_start)

            @pl.when(chip != bb)
            def _():
                hop(both_start)

    def step(i, carry):
        t, side, sc, hw, place = subslot(i + units)
        wave, b, valid = event(t, side, place)
        h = wave * (hh // 2) + hw

        @pl.when(jnp.logical_and(valid, place < n - 1))
        def _():
            q_hop(b, sc, h, z).wait_recv()
            q_hop(b, sc, h, z + 1 - 2 * side).start()

        @pl.when(jnp.logical_and(jnp.logical_and(t == 2 * place, place < n - 1), sc == c))
        def _():
            @pl.when(side == 0)
            def _():
                for half in range(2):
                    q_out(2, half, hh // 2 + hw).start()

            @pl.when(side == 1)
            def _():
                for half in range(2):
                    q_out(0, half, hh // 2 + hw).start()

        t, side, sc, hw, place = subslot(i)
        wave, b, valid = event(t, side, place)
        early = jnp.logical_and(side == 0, sc == c)
        is_first, is_last = t == -1, t == 2 * n - 2
        own = jnp.logical_or(is_first, is_last)
        wave = jnp.where(own, side, wave)
        b = jnp.where(own, z, b)
        valid = jnp.where(is_first, early, jnp.where(is_last, jnp.logical_not(early), valid))
        h = wave * (hh // 2) + hw

        @pl.when(valid)
        def _():
            @pl.when(jnp.where(own, sc != c, place == n - 1))
            def _():
                q_hop(b, sc, h, z).wait_recv()

            compute(b, sc, h)

            @pl.when(jnp.logical_and(own, sc != c))
            def _():
                both_start(*sib_out(h))

        @pl.when(t >= 0)
        def _():
            def one(w, carry):
                bs = jnp.where(w == 0, 2 * n - 3 - place - t, t - 2 * n + 2 + place)
                flow(bs, w, side, sc, hw, place)
                return carry

            lax.fori_loop(0, 2, one, 0)

        return carry

    lax.fori_loop(0, 2 * n * units, step, 0)

    def finish(i, carry):
        half = (i % 2 + c) % 2
        h = i // 2
        hd = half * hh + h
        acc[...] = tail[hd]
        acc_st[...] = tail_st[hd]

        @pl.when(half == c)
        def _():
            merge(acc, acc_st, part[z, c, h], part_st.at[z, c, h])

        @pl.when(half != c)
        def _():
            both_wait_recv(*sib_out(h))
            merge(acc, acc_st, sib[h], sib_st.at[h])

        def arrive(way):
            both_wait_recv(
                copy(snd.at[0, 0, 0], fin.at[way, half, h], s_send.at[0, 0, 0, 0], f_recv.at[0, way, half, h], z, c),
                copy(snd_st.at[0, 0, 0], fin_st.at[way, half, h], s_send.at[1, 0, 0, 0], f_recv.at[1, way, half, h], z, c),
            )
            merge(acc, acc_st, decode(fin.at[way, half, h], fin_st.at[way, half, h]), fin_st.at[way, half, h])

        @pl.when(jnp.logical_not(last))
        def _():
            arrive(0)

        @pl.when(jnp.logical_not(first))
        def _():
            arrive(1)

        out[hd] = jnp.transpose(acc[...] / acc_st[1:2, :]).astype(jnp.bfloat16)
        return carry

    lax.fori_loop(0, units, finish, 0)

    for one in kv_out():
        one.wait_send()
    for h in range(hh):
        both_wait_send(*sib_out(h))
        q_out(1, o, h).wait_send()

        @pl.when(jnp.logical_not(first))
        def _():
            for half in range(2):
                q_out(0, half, h).wait_send()

        @pl.when(jnp.logical_not(last))
        def _():
            for half in range(2):
                q_out(2, half, h).wait_send()

    def drain(i, carry):
        b, sc, h = i // units, (i // hh) % 2, i % hh

        @pl.when(b != z)
        def _():
            flow_out(b, sc, h, z, 0)[0](both_wait_send)

            @pl.when(jnp.where(b < z, jnp.logical_not(last), jnp.logical_not(first)))
            def _():
                q_hop(b, sc, h, z).wait_send()

        return carry

    lax.fori_loop(0, n * units, drain, 0)


def per_device_paired(
    n,
    queries,
    new_keys,
    step_new_values,
    context_keys,
    context_values,
    cluster_centroid_keys,
    cluster_mean_values,
    cluster_page_slot,
    picks,
):
    num_steps, rows, num_heads, head_width = queries.shape
    kv_local, tokens = context_keys.shape[:2]
    cl = cluster_centroid_keys.shape[1]
    ncl = cluster_page_slot.shape[1]
    if 2 * ncl > 128 or rows > 16 or 2 * cl > 16 or kv_local % 4:
        return per_device_plain(
            queries, new_keys, step_new_values, context_keys, context_values,
            cluster_centroid_keys, cluster_mean_values, cluster_page_slot, picks,
        )
    page = tokens // cl
    group = num_heads // kv_local
    hh = kv_local // 2
    nq = num_steps * rows * group
    bf16, f32, i16 = jnp.bfloat16, jnp.float32, jnp.int16
    q = queries.reshape(num_steps, rows, kv_local, group, head_width)
    q = q.transpose(2, 0, 1, 3, 4).reshape(kv_local, nq, head_width)
    chosen = jnp.pad(picks.transpose(1, 0, 2), ((0, 0), (0, 16 - rows), (0, 0)), constant_values=-1)
    slots = jnp.pad(cluster_page_slot, ((0, 0), (ncl, 128 - 2 * ncl)), constant_values=-1)[:, None, :]
    pad = ((0, 0), (0, 16 - cl), (0, 0))
    cents = jnp.pad(cluster_centroid_keys, pad).reshape(2, hh, 16, head_width)
    pad = ((0, 0), (0, 128 - cl), (0, 0))
    vx = jnp.concatenate([context_values, jnp.pad(cluster_mean_values, pad)], axis=1)
    vx = vx.transpose(0, 2, 1).reshape(2, hh, head_width, tokens + 128)
    nk = new_keys.transpose(2, 0, 1, 3).reshape(kv_local, num_steps * rows, head_width)
    nv = step_new_values.transpose(2, 0, 1, 3).reshape(kv_local, num_steps * rows, head_width)
    dims = (num_steps, rows, group, hh, cl, page, head_width, ncl)
    dma = pltpu.SemaphoreType.DMA
    vm = pltpu.VMEM
    unit = (n, 2, hh)
    out = pl.pallas_call(
        functools.partial(chain_kernel, n, dims),
        out_shape=jax.ShapeDtypeStruct((kv_local, nq, head_width), bf16),
        in_specs=[pl.BlockSpec(memory_space=pl.ANY if i == 1 else pltpu.VMEM) for i in range(8)],
        out_specs=pl.BlockSpec(memory_space=pltpu.VMEM),
        scratch_shapes=[
            vm((2, hh, nq + 16, head_width), bf16),
            vm(unit + (nq + 16, head_width), bf16),
            vm((2, hh, tokens + 16, head_width), bf16),
            vm(vx.shape, bf16),
            vm(unit + (head_width, nq), f32),
            vm(unit + (4, nq), f32),
            vm(unit + (head_width, nq), i16),
            vm(unit + (4, nq), f32),
            vm(unit + (head_width, nq), i16),
            vm(unit + (4, nq), f32),
            vm((2, 2, hh, head_width, nq), i16),
            vm((2, 2, hh, 4, nq), f32),
            vm((hh, head_width, nq), f32),
            vm((hh, 4, nq), f32),
            vm((kv_local, head_width, nq), f32),
            vm((kv_local, 4, nq), f32),
            vm((head_width, nq), f32),
            vm((4, nq), f32),
            vm((2, tokens + 128, nq), bf16),
            vm((2, tokens + 16, nq), f32),
            dma((3, 2, hh)),
            dma(unit),
            dma(unit),
            dma((2,) + unit),
            dma((2,) + unit),
            dma((2, 2, 2, hh)),
            dma((2, hh)),
            dma((2, hh)),
            dma((3,)),
            dma((3,)),
            dma,
        ],
        compiler_params=pltpu.CompilerParams(
            collective_id=0, has_side_effects=True, vmem_limit_bytes=40 * 1024 * 1024
        ),
        cost_estimate=pl.CostEstimate(
            flops=8 * n * 2 * kv_local * nq * tokens * head_width,
            bytes_accessed=8 * 1024 * 1024,
            transcendentals=2 * n * kv_local * nq * tokens,
        ),
    )(q, context_keys, cents, vx, chosen, slots, nk, nv)
    out = out.reshape(kv_local, num_steps, rows, group, head_width)
    return out.transpose(1, 2, 0, 3, 4).reshape(num_steps, rows, num_heads, head_width)


def solution(mesh):
    sizes = mesh.shape
    paired = sizes["row"] == 1 and sizes["ctx"] % 2 == 0 and sizes["ctx"] > 2
    step = functools.partial(per_device_paired, sizes["ctx"] // 2) if paired else per_device_plain
    return jax.shard_map(
        step,
        mesh=mesh,
        in_specs=(
            P(None, ("groups", "ctx", "row"), "rep", None),
            P(None, ("groups", "ctx", "row"), "rep", None),
            P(None, ("groups", "ctx", "row"), "rep", None),
            P("rep", ("groups", "ctx"), None),
            P("rep", ("groups", "ctx"), None),
            P("rep", ("groups", "ctx"), None),
            P("rep", ("groups", "ctx"), None),
            P("rep", "groups"),
            P(("groups", "ctx", "row"), "rep", None),
        ),
        out_specs=P(None, ("groups", "ctx", "row"), "rep", None),
        check_vma=False,
    )
```

```python
import functools
import math

import jax
import jax.numpy as jnp
from jax import lax
from jax.experimental import pallas as pl
from jax.experimental.pallas import tpu as pltpu
from jax.sharding import PartitionSpec as P

FLOOR_SCORE = -10000.0


def tail_block(queries, new_keys, step_new_values, logit_multiplier):
    num_steps, num_rows, num_heads, head_width = queries.shape
    kv_heads = new_keys.shape[2]
    grouped = queries.astype(jnp.float32).reshape(
        num_steps, num_rows, kv_heads, num_heads // kv_heads, head_width
    )
    scores = (
        jnp.einsum("srhgd,trhd->srhgt", grouped, new_keys.astype(jnp.float32)) * logit_multiplier
    )
    step_ids = jnp.arange(num_steps, dtype=jnp.int32)
    causal = (step_ids[None, :] <= step_ids[:, None])[:, None, None, None, :]
    block_top = jnp.max(jnp.where(causal, scores, FLOOR_SCORE), axis=-1)
    weights = jnp.where(causal, jnp.exp(scores - block_top[..., None]), 0.0)
    sum_total = jnp.sum(weights, axis=-1)
    rounded = weights.astype(jnp.bfloat16).astype(jnp.float32)
    tail_out = jnp.einsum("srhgt,trhd->srhgd", rounded, step_new_values.astype(jnp.float32))
    return (
        tail_out.reshape(num_steps, num_rows, num_heads, head_width),
        sum_total.reshape(num_steps, num_rows, num_heads),
        block_top.reshape(num_steps, num_rows, num_heads),
    )


def per_device_plain(
    queries,
    new_keys,
    step_new_values,
    context_keys,
    context_values,
    cluster_centroid_keys,
    cluster_mean_values,
    cluster_page_slot,
    picks,
):
    num_steps = queries.shape[0]
    num_heads = queries.shape[2]
    head_width = queries.shape[3]
    kv_local = context_keys.shape[0]
    span_tokens = context_keys.shape[1]
    cl_local = cluster_centroid_keys.shape[1]
    grouping_member_entries = span_tokens // cl_local
    query_group_size = num_heads // kv_local
    logit_multiplier = 1.0 / math.sqrt(head_width)
    membership_log_weight = math.log(grouping_member_entries)
    shard_index = lax.axis_index("ctx")
    gathered = lax.all_gather(queries, "ctx", axis=1, tiled=True)
    chosen = lax.all_gather(picks, "ctx", axis=0, tiled=True)
    rows_all = gathered.shape[1]
    cluster_ids = jnp.arange(cluster_page_slot.shape[1], dtype=jnp.int32)
    pick_hits = chosen[..., None] == cluster_ids
    picked_slots = jnp.sum(jnp.where(pick_hits, cluster_page_slot[None, :, None, :], 0), axis=-1)
    local_ids = shard_index * cl_local + jnp.arange(cl_local, dtype=jnp.int32)
    slot_used = jnp.any(picked_slots[..., None] == local_ids, axis=2)
    cluster_used = jnp.any(chosen[..., None] == local_ids, axis=2)
    step_outs, step_totals, step_tops = ([], [], [])
    for step_index in range(num_steps):
        head_outs, head_totals, head_tops = ([], [], [])
        for current_head_index in range(kv_local):
            generation_probe_vectors = gathered[
                step_index,
                :,
                current_head_index * query_group_size : (current_head_index + 1) * query_group_size,
                :,
            ].reshape(rows_all * query_group_size, head_width)
            exact_mask = slot_used[:, current_head_index][:, None, :, None]
            coarse_mask = jnp.logical_not(cluster_used[:, current_head_index])[:, None, :]
            exact_scores = (
                jnp.einsum(
                    "qd,kd->qk",
                    generation_probe_vectors,
                    context_keys[current_head_index],
                    preferred_element_type=jnp.float32,
                )
                * logit_multiplier
            )
            exact_scores = exact_scores.reshape(
                rows_all, query_group_size, cl_local, grouping_member_entries
            )
            prototype_logits = (
                jnp.einsum(
                    "qd,kd->qk",
                    generation_probe_vectors,
                    cluster_centroid_keys[current_head_index],
                    preferred_element_type=jnp.float32,
                )
                * logit_multiplier
                + membership_log_weight
            )
            prototype_logits = prototype_logits.reshape(rows_all, query_group_size, cl_local)
            block_top = jnp.maximum(
                jnp.max(jnp.where(exact_mask, exact_scores, FLOOR_SCORE), axis=(2, 3)),
                jnp.max(jnp.where(coarse_mask, prototype_logits, FLOOR_SCORE), axis=2),
            )
            exact_weights = jnp.where(
                exact_mask, jnp.exp(exact_scores - block_top[:, :, None, None]), 0.0
            )
            coarse_weights = jnp.where(
                coarse_mask, jnp.exp(prototype_logits - block_top[:, :, None]), 0.0
            )
            sum_total = jnp.sum(exact_weights, axis=(2, 3)) + jnp.sum(coarse_weights, axis=2)
            block_out = jnp.dot(
                exact_weights.astype(jnp.bfloat16).reshape(
                    rows_all * query_group_size, span_tokens
                ),
                context_values[current_head_index],
                preferred_element_type=jnp.float32,
            )
            block_out = block_out + jnp.dot(
                coarse_weights.astype(jnp.bfloat16).reshape(rows_all * query_group_size, cl_local),
                cluster_mean_values[current_head_index],
                preferred_element_type=jnp.float32,
            )
            head_outs.append(block_out.reshape(rows_all, query_group_size, head_width))
            head_totals.append(sum_total)
            head_tops.append(block_top)
        step_outs.append(jnp.concatenate(head_outs, axis=1))
        step_totals.append(jnp.concatenate(head_totals, axis=1))
        step_tops.append(jnp.concatenate(head_tops, axis=1))
    partial_outs = jnp.stack(step_outs)
    partial_totals = jnp.stack(step_totals)
    partial_tops = jnp.stack(step_tops)
    got_tops, got_totals, got_outs = (
        lax.all_to_all(partial_tops[None], "ctx", split_axis=2, concat_axis=0, tiled=True),
        lax.all_to_all(partial_totals[None], "ctx", split_axis=2, concat_axis=0, tiled=True),
        lax.all_to_all(partial_outs[None], "ctx", split_axis=2, concat_axis=0, tiled=True),
    )
    best_top = jnp.max(got_tops, axis=0)
    factor = jnp.exp(got_tops - best_top)
    sum_total = jnp.sum(factor * got_totals, axis=0)
    merged = jnp.sum(factor[..., None] * got_outs, axis=0)
    tail_out, tail_total, tail_top = tail_block(
        queries, new_keys, step_new_values, logit_multiplier
    )
    overall = jnp.maximum(best_top, tail_top)
    context_factor = jnp.exp(best_top - overall)
    tail_factor = jnp.exp(tail_top - overall)
    numer = context_factor[..., None] * merged + tail_factor[..., None] * tail_out
    denom = context_factor * sum_total + tail_factor * tail_total
    return (numer / denom[..., None]).astype(jnp.bfloat16)


MESH = pl.DeviceIdType.MESH
LOG2E = math.log2(math.e)
NT = (((1,), (1,)), ((), ()))
TN = (((0,), (0,)), ((), ()))


def chain_kernel(
    n, dims,
    queries, keys, cents, vals, means, picks, slots, nk, nv, out,
    qx,
    qbuf, kb, vr, vb, part, part_st, inc, inc_st, snd, snd_st, fin, fin_st, sib, sib_st,
    tail, tail_st, acc, acc_st, wbuf, score,
    q_send, f_send, q_recv, s_send, s_recv, f_recv, b_send, b_recv, kv_send, kv_recv, k_sem,
):
    num_steps, rows, group, hh, cl, page, head_width, ncl = dims
    nq = num_steps * rows * group
    units = 2 * hh
    me = lax.axis_index("ctx")
    z, c = me // 2, me % 2
    o = 1 - c
    first, last = z == 0, z == n - 1
    scale2 = LOG2E / math.sqrt(head_width)
    coarse2 = LOG2E * math.log(page)
    floor2 = FLOOR_SCORE * LOG2E
    tokens = cl * page
    num_picks = picks.shape[2]

    def copy(src, dst, send, recv, chip, core):
        return pltpu.make_async_remote_copy(
            src_ref=src, dst_ref=dst, send_sem=send, recv_sem=recv,
            device_id={"ctx": chip * 2 + core}, device_id_type=MESH,
        )

    barrier = pltpu.get_barrier_semaphore()
    pl.semaphore_signal(barrier, inc=1, device_id={"ctx": z * 2 + o}, device_id_type=MESH)

    @pl.when(jnp.logical_not(first))
    def _():
        for core in range(2):
            pl.semaphore_signal(barrier, inc=1, device_id={"ctx": (z - 1) * 2 + core}, device_id_type=MESH)

    @pl.when(jnp.logical_not(last))
    def _():
        for core in range(2):
            pl.semaphore_signal(barrier, inc=1, device_id={"ctx": (z + 1) * 2 + core}, device_id_type=MESH)

    own_keys = pltpu.make_async_copy(keys.at[pl.ds(c * hh, hh)], kb.at[c, :, 0:tokens, :], k_sem.at[0])
    own_keys.start()
    own_vals = pltpu.make_async_copy(vals.at[pl.ds(c * hh, hh)], vr.at[c, :, 0:tokens, :], k_sem.at[1])
    own_vals.start()

    def iota(shape, axis):
        return lax.broadcasted_iota(jnp.int32, shape, axis)

    page_of = jnp.where(slots[...] == iota((2 * hh, 128, 128), 1), 1.0, 0.0).astype(jnp.bfloat16)
    lane = iota((16, 128), 1)
    for hd in range(2 * hh):
        ids = picks[hd] + ncl
        used = jnp.zeros((16, 128), jnp.float32)
        for k in range(num_picks):
            used = jnp.where(ids[:, k : k + 1] == lane, 1.0, used)
        pages = lax.dot_general(used.astype(jnp.bfloat16), page_of[hd], NT, preferred_element_type=jnp.float32)
        coarse = jnp.where(jnp.logical_and(lane >= ncl, lane < 2 * ncl), 1.0 - used, 0.0)
        qx[hd // hh, hd % hh, 0:nq, :] = queries[hd]
        qx[hd // hh, hd % hh, nq : nq + 16, :] = (pages + coarse).astype(jnp.bfloat16)

    pl.semaphore_wait(barrier, 5 - 2 * first.astype(jnp.int32) - 2 * last.astype(jnp.int32))

    def q_out(way, half, h):
        chip = (z - 1, z, z + 1)[way]
        return copy(qx.at[half, h], qbuf.at[z, c, h], q_send.at[way, half, h], q_recv.at[z, c, h], chip, half)

    def q_hop(b, sc, h, chip):
        ref = qbuf.at[b, sc, h]
        return copy(ref, ref, f_send.at[b, sc, h], q_recv.at[b, sc, h], chip, c)

    def kv_out():
        return (
            copy(
                keys.at[pl.ds(o * hh, hh)], kb.at[c, :, 0:tokens, :], kv_send.at[0], kv_recv.at[0], z, o
            ),
            copy(cents.at[o], kb.at[c, :, tokens : tokens + 16, :], kv_send.at[2], kv_recv.at[2], z, o),
            copy(
                vals.at[pl.ds(o * hh, hh)], vr.at[c, :, 0:tokens, :], kv_send.at[1], kv_recv.at[1], z, o
            ),
            copy(
                means.at[o], vr.at[c, :, tokens : tokens + 128, :], kv_send.at[3], kv_recv.at[3], z, o
            ),
        )

    for h in range(hh // 2):

        @pl.when(jnp.logical_not(first))
        def _():
            for half in range(2):
                q_out(0, half, h).start()

        @pl.when(jnp.logical_not(last))
        def _():
            for half in range(2):
                q_out(2, half, h).start()

    for one in kv_out():
        one.start()

    for h in range(hh):
        q_out(1, o, h).start()

    kb[c, :, tokens : tokens + 16, :] = cents[c]
    vr[c, :, tokens : tokens + 128, :] = means[c]
    qbuf[z, c] = qx[c]
    wbuf[...] = jnp.zeros_like(wbuf)

    def tail_head(hd, carry):
        q = qx[hd // hh, hd % hh, 0:nq, :]
        s = lax.dot_general(nk[hd], q, NT, preferred_element_type=jnp.float32) * scale2
        shape = (num_steps * rows, nq)
        t, r = iota(shape, 0) // rows, iota(shape, 0) % rows
        lane = iota(shape, 1)
        seen = jnp.logical_and((lane // group) % rows == r, t <= lane // (rows * group))
        s = jnp.where(seen, s, floor2)
        top = jnp.max(s, axis=0, keepdims=True)
        w = jnp.where(seen, jnp.exp2(s - top), 0.0)
        tail_st[hd, 0:1, :] = top
        tail_st[hd, 1:2, :] = jnp.sum(w, axis=0, keepdims=True)
        tail[hd] = lax.dot_general(nv[hd], w.astype(jnp.bfloat16), TN, preferred_element_type=jnp.float32)
        return carry

    lax.fori_loop(0, 2 * hh, tail_head, 0)

    sel_rows = 48
    si, sl = iota((sel_rows, 128), 0), iota((sel_rows, 128), 1)
    in_page = si < 2 * cl
    blk = jnp.where(si >= 32, 1, 0)
    j = si - 16 - 16 * blk
    in_coarse = jnp.logical_and(si >= 16, j < cl)
    target = jnp.where(in_page, z * 2 * cl + si, jnp.where(in_coarse, ncl + (z * 2 + blk) * cl + j, -1))
    select = jnp.where(sl == target, 1.0, 0.0).astype(jnp.bfloat16)
    spread = jnp.where((iota((16, nq), 1) // group) % rows == iota((16, nq), 0), 1.0, 0.0).astype(jnp.bfloat16)

    own_keys.wait()
    own_vals.wait()
    for one in kv_out():
        one.wait_recv()

    def turn(i, carry):
        vb[i // hh, i % hh] = jnp.transpose(vr[i // hh, i % hh])
        return carry

    lax.fori_loop(0, 2 * hh, turn, 0)

    def compute(b, sc, h):
        q = qbuf[b, sc, h, 0:nq, :]
        bits = qbuf[b, sc, h, nq : nq + 16, :]
        flags = lax.dot_general(select, bits, NT, preferred_element_type=jnp.float32)
        flags = jnp.dot(flags.astype(jnp.bfloat16), spread, preferred_element_type=jnp.float32)
        outs = []
        for d in range(2):
            score[d] = lax.dot_general(kb[d, h], q, NT, preferred_element_type=jnp.float32) * scale2
        for d in range(2):
            coarse_on = flags[16 + 16 * d : 32 + 16 * d, :] > 0.5
            coarse = score[d, tokens : tokens + 16, :] + coarse2
            top = jnp.max(jnp.where(coarse_on, coarse, floor2), axis=0, keepdims=True)
            on = [flags[d * cl + p : d * cl + p + 1, :] > 0.5 for p in range(cl)]
            for p in range(cl):
                page_top = jnp.max(score[d, p * page : (p + 1) * page, :], axis=0, keepdims=True)
                top = jnp.maximum(top, jnp.where(on[p], page_top, floor2))
            wc = jnp.where(coarse_on, jnp.exp2(coarse - top), 0.0)
            wbuf[d, tokens : tokens + 16, :] = wc.astype(jnp.bfloat16)
            total = jnp.sum(wc, axis=0, keepdims=True)
            for p in range(cl):
                w = jnp.exp2(score[d, p * page : (p + 1) * page, :] - jnp.where(on[p], top, 1e30))
                wbuf[d, p * page : (p + 1) * page, :] = w.astype(jnp.bfloat16)
                total = total + jnp.sum(w, axis=0, keepdims=True)
            outs.append((jnp.dot(vb[d, h], wbuf[d], preferred_element_type=jnp.float32), total, top))
        (o0, l0, m0), (o1, l1, m1) = outs
        top = jnp.maximum(m0, m1)
        a0, a1 = jnp.exp2(m0 - top), jnp.exp2(m1 - top)
        part[b, sc, h] = a0 * o0 + a1 * o1
        part_st[b, sc, h, 0:1, :] = top
        part_st[b, sc, h, 1:2, :] = a0 * l0 + a1 * l1

    def merge(o_ref, st_ref, values, st):
        m0, m1 = st_ref[0:1, :], st[0:1, :]
        top = jnp.maximum(m0, m1)
        a0, a1 = jnp.exp2(m0 - top), jnp.exp2(m1 - top)
        o_ref[...] = a0 * o_ref[...] + a1 * values
        st_ref[1:2, :] = a0 * st_ref[1:2, :] + a1 * st[1:2, :]
        st_ref[0:1, :] = top

    def decode(ref, st_ref):
        return ref[...].astype(jnp.int32).astype(jnp.float32) * st_ref[2:3, :]

    def flow_out(b, sc, h, chip, way):
        def hop(fn):
            fn(
                copy(snd.at[b, sc, h], inc.at[b, sc, h], s_send.at[0, b, sc, h], s_recv.at[0, b, sc, h], chip, c),
                copy(snd_st.at[b, sc, h], inc_st.at[b, sc, h], s_send.at[1, b, sc, h], s_recv.at[1, b, sc, h], chip, c),
            )

        def home(fn):
            fn(
                copy(snd.at[b, sc, h], fin.at[way, c, h], s_send.at[0, b, sc, h], f_recv.at[0, way, c, h], b, sc),
                copy(snd_st.at[b, sc, h], fin_st.at[way, c, h], s_send.at[1, b, sc, h], f_recv.at[1, way, c, h], b, sc),
            )

        return hop, home

    def both_start(x, y):
        x.start()
        y.start()

    def both_wait_send(x, y):
        x.wait_send()
        y.wait_send()

    def both_wait_recv(x, y):
        x.wait_recv()
        y.wait_recv()

    def sib_out(h):
        return (
            copy(part.at[z, o, h], sib.at[h], b_send.at[0, h], b_recv.at[0, h], z, o),
            copy(part_st.at[z, o, h], sib_st.at[h], b_send.at[1, h], b_recv.at[1, h], z, o),
        )

    def subslot(i):
        k = i % units
        side = k % 2
        place = jnp.where(side == 0, z, n - 1 - z)
        return i // units - 1, side, (k // 2 + c) % 2, k // 4, place

    def event(t, side, place):
        wave = jnp.where(t < place, 0, 1)
        dist = jnp.where(t < place, t + 1, 2 * place - t)
        valid = jnp.logical_and(t >= 0, t < 2 * place)
        return wave, jnp.clip(z + (2 * side - 1) * dist, 0, n - 1), valid

    def flow(bs, wave, side, sc, hw, place):
        @pl.when(jnp.logical_and(bs >= 0, bs < place))
        def _():
            bb = jnp.clip(jnp.where(side == 0, bs, n - 1 - bs), 0, n - 1)
            h = wave * (hh // 2) + hw
            o_ref, st_ref = part.at[bb, sc, h], part_st.at[bb, sc, h]

            @pl.when(place < n - 1)
            def _():
                flow_out(bb, sc, h, z, side)[0](both_wait_recv)
                merge(o_ref, st_ref, decode(inc.at[bb, sc, h], inc_st.at[bb, sc, h]), inc_st.at[bb, sc, h])

            values = o_ref[...]
            size = jnp.maximum(jnp.max(jnp.abs(values), axis=0, keepdims=True), 1e-30)
            snd[bb, sc, h] = jnp.round(values * (32767.0 / size)).astype(jnp.int32).astype(jnp.int16)
            snd_st[bb, sc, h, 0:2, :] = st_ref[0:2, :]
            snd_st[bb, sc, h, 2:3, :] = size * (1.0 / 32767.0)
            chip = z + 2 * side - 1
            hop, home = flow_out(bb, sc, h, chip, side)

            @pl.when(chip == bb)
            def _():
                home(both_start)

            @pl.when(chip != bb)
            def _():
                hop(both_start)

    def step(i, carry):
        t, side, sc, hw, place = subslot(i + units)
        wave, b, valid = event(t, side, place)
        h = wave * (hh // 2) + hw

        @pl.when(jnp.logical_and(valid, place < n - 1))
        def _():
            q_hop(b, sc, h, z).wait_recv()
            q_hop(b, sc, h, z + 1 - 2 * side).start()

        @pl.when(jnp.logical_and(jnp.logical_and(t == 2 * place, place < n - 1), sc == c))
        def _():
            @pl.when(side == 0)
            def _():
                for half in range(2):
                    q_out(2, half, hh // 2 + hw).start()

            @pl.when(side == 1)
            def _():
                for half in range(2):
                    q_out(0, half, hh // 2 + hw).start()

        t, side, sc, hw, place = subslot(i)
        wave, b, valid = event(t, side, place)
        early = jnp.logical_and(side == 0, sc == c)
        is_first, is_last = t == -1, t == 2 * n - 2
        own = jnp.logical_or(is_first, is_last)
        wave = jnp.where(own, side, wave)
        b = jnp.where(own, z, b)
        valid = jnp.where(is_first, early, jnp.where(is_last, jnp.logical_not(early), valid))
        h = wave * (hh // 2) + hw

        @pl.when(valid)
        def _():
            @pl.when(jnp.where(own, sc != c, place == n - 1))
            def _():
                q_hop(b, sc, h, z).wait_recv()

            compute(b, sc, h)

            @pl.when(jnp.logical_and(own, sc != c))
            def _():
                both_start(*sib_out(h))

        @pl.when(t >= 0)
        def _():
            def one(w, carry):
                bs = jnp.where(w == 0, 2 * n - 3 - place - t, t - 2 * n + 2 + place)
                flow(bs, w, side, sc, hw, place)
                return carry

            lax.fori_loop(0, 2, one, 0)

        return carry

    lax.fori_loop(0, 2 * n * units, step, 0)

    def finish(i, carry):
        half = (i % 2 + c) % 2
        h = i // 2
        hd = half * hh + h
        acc[...] = tail[hd]
        acc_st[...] = tail_st[hd]

        @pl.when(half == c)
        def _():
            merge(acc, acc_st, part[z, c, h], part_st.at[z, c, h])

        @pl.when(half != c)
        def _():
            both_wait_recv(*sib_out(h))
            merge(acc, acc_st, sib[h], sib_st.at[h])

        def arrive(way):
            both_wait_recv(
                copy(snd.at[0, 0, 0], fin.at[way, half, h], s_send.at[0, 0, 0, 0], f_recv.at[0, way, half, h], z, c),
                copy(snd_st.at[0, 0, 0], fin_st.at[way, half, h], s_send.at[1, 0, 0, 0], f_recv.at[1, way, half, h], z, c),
            )
            merge(acc, acc_st, decode(fin.at[way, half, h], fin_st.at[way, half, h]), fin_st.at[way, half, h])

        @pl.when(jnp.logical_not(last))
        def _():
            arrive(0)

        @pl.when(jnp.logical_not(first))
        def _():
            arrive(1)

        out[hd] = jnp.transpose(acc[...] / acc_st[1:2, :]).astype(jnp.bfloat16)
        return carry

    lax.fori_loop(0, units, finish, 0)

    for one in kv_out():
        one.wait_send()
    for h in range(hh):
        both_wait_send(*sib_out(h))
        q_out(1, o, h).wait_send()

        @pl.when(jnp.logical_not(first))
        def _():
            for half in range(2):
                q_out(0, half, h).wait_send()

        @pl.when(jnp.logical_not(last))
        def _():
            for half in range(2):
                q_out(2, half, h).wait_send()

    def drain(i, carry):
        b, sc, h = i // units, (i // hh) % 2, i % hh

        @pl.when(b != z)
        def _():
            flow_out(b, sc, h, z, 0)[0](both_wait_send)

            @pl.when(jnp.where(b < z, jnp.logical_not(last), jnp.logical_not(first)))
            def _():
                q_hop(b, sc, h, z).wait_send()

        return carry

    lax.fori_loop(0, n * units, drain, 0)


def per_device_paired(
    n,
    queries,
    new_keys,
    step_new_values,
    context_keys,
    context_values,
    cluster_centroid_keys,
    cluster_mean_values,
    cluster_page_slot,
    picks,
):
    num_steps, rows, num_heads, head_width = queries.shape
    kv_local, tokens = context_keys.shape[:2]
    cl = cluster_centroid_keys.shape[1]
    ncl = cluster_page_slot.shape[1]
    if 2 * ncl > 128 or rows > 16 or 2 * cl > 16 or kv_local % 4:
        return per_device_plain(
            queries, new_keys, step_new_values, context_keys, context_values,
            cluster_centroid_keys, cluster_mean_values, cluster_page_slot, picks,
        )
    page = tokens // cl
    group = num_heads // kv_local
    hh = kv_local // 2
    nq = num_steps * rows * group
    bf16, f32, i16 = jnp.bfloat16, jnp.float32, jnp.int16
    q = queries.reshape(num_steps, rows, kv_local, group, head_width)
    q = q.transpose(2, 0, 1, 3, 4).reshape(kv_local, nq, head_width)
    chosen = jnp.pad(picks.transpose(1, 0, 2), ((0, 0), (0, 16 - rows), (0, 0)), constant_values=-1)
    slots = jnp.pad(cluster_page_slot, ((0, 0), (ncl, 128 - 2 * ncl)), constant_values=-1)[:, None, :]
    pad = ((0, 0), (0, 16 - cl), (0, 0))
    cents = jnp.pad(cluster_centroid_keys, pad).reshape(2, hh, 16, head_width)
    pad = ((0, 0), (0, 128 - cl), (0, 0))
    means = jnp.pad(cluster_mean_values, pad).reshape(2, hh, 128, head_width)
    nk = new_keys.transpose(2, 0, 1, 3).reshape(kv_local, num_steps * rows, head_width)
    nv = step_new_values.transpose(2, 0, 1, 3).reshape(kv_local, num_steps * rows, head_width)
    dims = (num_steps, rows, group, hh, cl, page, head_width, ncl)
    dma = pltpu.SemaphoreType.DMA
    vm = pltpu.VMEM
    unit = (n, 2, hh)
    out = pl.pallas_call(
        functools.partial(chain_kernel, n, dims),
        out_shape=jax.ShapeDtypeStruct((kv_local, nq, head_width), bf16),
        in_specs=[pl.BlockSpec(memory_space=pl.ANY if i in (1, 3) else pltpu.VMEM) for i in range(9)],
        out_specs=pl.BlockSpec(memory_space=pltpu.VMEM),
        scratch_shapes=[
            vm((2, hh, nq + 16, head_width), bf16),
            vm(unit + (nq + 16, head_width), bf16),
            vm((2, hh, tokens + 16, head_width), bf16),
            vm((2, hh, tokens + 128, head_width), bf16),
            vm((2, hh, head_width, tokens + 128), bf16),
            vm(unit + (head_width, nq), f32),
            vm(unit + (4, nq), f32),
            vm(unit + (head_width, nq), i16),
            vm(unit + (4, nq), f32),
            vm(unit + (head_width, nq), i16),
            vm(unit + (4, nq), f32),
            vm((2, 2, hh, head_width, nq), i16),
            vm((2, 2, hh, 4, nq), f32),
            vm((hh, head_width, nq), f32),
            vm((hh, 4, nq), f32),
            vm((kv_local, head_width, nq), f32),
            vm((kv_local, 4, nq), f32),
            vm((head_width, nq), f32),
            vm((4, nq), f32),
            vm((2, tokens + 128, nq), bf16),
            vm((2, tokens + 16, nq), f32),
            dma((3, 2, hh)),
            dma(unit),
            dma(unit),
            dma((2,) + unit),
            dma((2,) + unit),
            dma((2, 2, 2, hh)),
            dma((2, hh)),
            dma((2, hh)),
            dma((4,)),
            dma((4,)),
            dma((2,)),
        ],
        compiler_params=pltpu.CompilerParams(
            collective_id=0, has_side_effects=True, vmem_limit_bytes=40 * 1024 * 1024
        ),
        cost_estimate=pl.CostEstimate(
            flops=8 * n * 2 * kv_local * nq * tokens * head_width,
            bytes_accessed=8 * 1024 * 1024,
            transcendentals=2 * n * kv_local * nq * tokens,
        ),
    )(q, context_keys, cents, context_values, means, chosen, slots, nk, nv)
    out = out.reshape(kv_local, num_steps, rows, group, head_width)
    return out.transpose(1, 2, 0, 3, 4).reshape(num_steps, rows, num_heads, head_width)


def solution(mesh):
    sizes = mesh.shape
    paired = sizes["row"] == 1 and sizes["ctx"] % 2 == 0 and sizes["ctx"] > 2
    step = functools.partial(per_device_paired, sizes["ctx"] // 2) if paired else per_device_plain
    return jax.shard_map(
        step,
        mesh=mesh,
        in_specs=(
            P(None, ("groups", "ctx", "row"), "rep", None),
            P(None, ("groups", "ctx", "row"), "rep", None),
            P(None, ("groups", "ctx", "row"), "rep", None),
            P("rep", ("groups", "ctx"), None),
            P("rep", ("groups", "ctx"), None),
            P("rep", ("groups", "ctx"), None),
            P("rep", ("groups", "ctx"), None),
            P("rep", "groups"),
            P(("groups", "ctx", "row"), "rep", None),
        ),
        out_specs=P(None, ("groups", "ctx", "row"), "rep", None),
        check_vma=False,
    )
```

```python
import functools
import math

import jax
import jax.numpy as jnp
from jax import lax
from jax.experimental import pallas as pl
from jax.experimental.pallas import tpu as pltpu
from jax.sharding import PartitionSpec as P

FLOOR_SCORE = -10000.0


def tail_block(queries, new_keys, step_new_values, logit_multiplier):
    num_steps, num_rows, num_heads, head_width = queries.shape
    kv_heads = new_keys.shape[2]
    grouped = queries.astype(jnp.float32).reshape(
        num_steps, num_rows, kv_heads, num_heads // kv_heads, head_width
    )
    scores = (
        jnp.einsum("srhgd,trhd->srhgt", grouped, new_keys.astype(jnp.float32)) * logit_multiplier
    )
    step_ids = jnp.arange(num_steps, dtype=jnp.int32)
    causal = (step_ids[None, :] <= step_ids[:, None])[:, None, None, None, :]
    block_top = jnp.max(jnp.where(causal, scores, FLOOR_SCORE), axis=-1)
    weights = jnp.where(causal, jnp.exp(scores - block_top[..., None]), 0.0)
    sum_total = jnp.sum(weights, axis=-1)
    rounded = weights.astype(jnp.bfloat16).astype(jnp.float32)
    tail_out = jnp.einsum("srhgt,trhd->srhgd", rounded, step_new_values.astype(jnp.float32))
    return (
        tail_out.reshape(num_steps, num_rows, num_heads, head_width),
        sum_total.reshape(num_steps, num_rows, num_heads),
        block_top.reshape(num_steps, num_rows, num_heads),
    )


def per_device_plain(
    queries,
    new_keys,
    step_new_values,
    context_keys,
    context_values,
    cluster_centroid_keys,
    cluster_mean_values,
    cluster_page_slot,
    picks,
):
    num_steps = queries.shape[0]
    num_heads = queries.shape[2]
    head_width = queries.shape[3]
    kv_local = context_keys.shape[0]
    span_tokens = context_keys.shape[1]
    cl_local = cluster_centroid_keys.shape[1]
    grouping_member_entries = span_tokens // cl_local
    query_group_size = num_heads // kv_local
    logit_multiplier = 1.0 / math.sqrt(head_width)
    membership_log_weight = math.log(grouping_member_entries)
    shard_index = lax.axis_index("ctx")
    gathered = lax.all_gather(queries, "ctx", axis=1, tiled=True)
    chosen = lax.all_gather(picks, "ctx", axis=0, tiled=True)
    rows_all = gathered.shape[1]
    cluster_ids = jnp.arange(cluster_page_slot.shape[1], dtype=jnp.int32)
    pick_hits = chosen[..., None] == cluster_ids
    picked_slots = jnp.sum(jnp.where(pick_hits, cluster_page_slot[None, :, None, :], 0), axis=-1)
    local_ids = shard_index * cl_local + jnp.arange(cl_local, dtype=jnp.int32)
    slot_used = jnp.any(picked_slots[..., None] == local_ids, axis=2)
    cluster_used = jnp.any(chosen[..., None] == local_ids, axis=2)
    step_outs, step_totals, step_tops = ([], [], [])
    for step_index in range(num_steps):
        head_outs, head_totals, head_tops = ([], [], [])
        for current_head_index in range(kv_local):
            generation_probe_vectors = gathered[
                step_index,
                :,
                current_head_index * query_group_size : (current_head_index + 1) * query_group_size,
                :,
            ].reshape(rows_all * query_group_size, head_width)
            exact_mask = slot_used[:, current_head_index][:, None, :, None]
            coarse_mask = jnp.logical_not(cluster_used[:, current_head_index])[:, None, :]
            exact_scores = (
                jnp.einsum(
                    "qd,kd->qk",
                    generation_probe_vectors,
                    context_keys[current_head_index],
                    preferred_element_type=jnp.float32,
                )
                * logit_multiplier
            )
            exact_scores = exact_scores.reshape(
                rows_all, query_group_size, cl_local, grouping_member_entries
            )
            prototype_logits = (
                jnp.einsum(
                    "qd,kd->qk",
                    generation_probe_vectors,
                    cluster_centroid_keys[current_head_index],
                    preferred_element_type=jnp.float32,
                )
                * logit_multiplier
                + membership_log_weight
            )
            prototype_logits = prototype_logits.reshape(rows_all, query_group_size, cl_local)
            block_top = jnp.maximum(
                jnp.max(jnp.where(exact_mask, exact_scores, FLOOR_SCORE), axis=(2, 3)),
                jnp.max(jnp.where(coarse_mask, prototype_logits, FLOOR_SCORE), axis=2),
            )
            exact_weights = jnp.where(
                exact_mask, jnp.exp(exact_scores - block_top[:, :, None, None]), 0.0
            )
            coarse_weights = jnp.where(
                coarse_mask, jnp.exp(prototype_logits - block_top[:, :, None]), 0.0
            )
            sum_total = jnp.sum(exact_weights, axis=(2, 3)) + jnp.sum(coarse_weights, axis=2)
            block_out = jnp.dot(
                exact_weights.astype(jnp.bfloat16).reshape(
                    rows_all * query_group_size, span_tokens
                ),
                context_values[current_head_index],
                preferred_element_type=jnp.float32,
            )
            block_out = block_out + jnp.dot(
                coarse_weights.astype(jnp.bfloat16).reshape(rows_all * query_group_size, cl_local),
                cluster_mean_values[current_head_index],
                preferred_element_type=jnp.float32,
            )
            head_outs.append(block_out.reshape(rows_all, query_group_size, head_width))
            head_totals.append(sum_total)
            head_tops.append(block_top)
        step_outs.append(jnp.concatenate(head_outs, axis=1))
        step_totals.append(jnp.concatenate(head_totals, axis=1))
        step_tops.append(jnp.concatenate(head_tops, axis=1))
    partial_outs = jnp.stack(step_outs)
    partial_totals = jnp.stack(step_totals)
    partial_tops = jnp.stack(step_tops)
    got_tops, got_totals, got_outs = (
        lax.all_to_all(partial_tops[None], "ctx", split_axis=2, concat_axis=0, tiled=True),
        lax.all_to_all(partial_totals[None], "ctx", split_axis=2, concat_axis=0, tiled=True),
        lax.all_to_all(partial_outs[None], "ctx", split_axis=2, concat_axis=0, tiled=True),
    )
    best_top = jnp.max(got_tops, axis=0)
    factor = jnp.exp(got_tops - best_top)
    sum_total = jnp.sum(factor * got_totals, axis=0)
    merged = jnp.sum(factor[..., None] * got_outs, axis=0)
    tail_out, tail_total, tail_top = tail_block(
        queries, new_keys, step_new_values, logit_multiplier
    )
    overall = jnp.maximum(best_top, tail_top)
    context_factor = jnp.exp(best_top - overall)
    tail_factor = jnp.exp(tail_top - overall)
    numer = context_factor[..., None] * merged + tail_factor[..., None] * tail_out
    denom = context_factor * sum_total + tail_factor * tail_total
    return (numer / denom[..., None]).astype(jnp.bfloat16)


MESH = pl.DeviceIdType.MESH
LOG2E = math.log2(math.e)
NT = (((1,), (1,)), ((), ()))
TN = (((0,), (0,)), ((), ()))


def chain_kernel(
    n, dims,
    queries, keys, cents, vx, picks, slots, nk, nv, out,
    qx,
    qbuf, kb, vb, part, part_st, inc, inc_st, snd, snd_st, fin, fin_st, sib, sib_st,
    tail, tail_st, acc, acc_st, wbuf, score,
    q_send, f_send, q_recv, s_send, s_recv, f_recv, b_send, b_recv, kv_send, kv_recv, k_sem,
):
    num_steps, rows, group, hh, cl, page, head_width, ncl = dims
    nq = num_steps * rows * group
    units = 2 * hh
    me = lax.axis_index("ctx")
    z, c = me // 2, me % 2
    o = 1 - c
    first, last = z == 0, z == n - 1
    scale2 = LOG2E / math.sqrt(head_width)
    coarse2 = LOG2E * math.log(page)
    floor2 = FLOOR_SCORE * LOG2E
    tokens = cl * page
    num_picks = picks.shape[2]

    def copy(src, dst, send, recv, chip, core):
        return pltpu.make_async_remote_copy(
            src_ref=src, dst_ref=dst, send_sem=send, recv_sem=recv,
            device_id={"ctx": chip * 2 + core}, device_id_type=MESH,
        )

    barrier = pltpu.get_barrier_semaphore()
    pl.semaphore_signal(barrier, inc=1, device_id={"ctx": z * 2 + o}, device_id_type=MESH)

    @pl.when(jnp.logical_not(first))
    def _():
        for core in range(2):
            pl.semaphore_signal(barrier, inc=1, device_id={"ctx": (z - 1) * 2 + core}, device_id_type=MESH)

    @pl.when(jnp.logical_not(last))
    def _():
        for core in range(2):
            pl.semaphore_signal(barrier, inc=1, device_id={"ctx": (z + 1) * 2 + core}, device_id_type=MESH)

    own_keys = pltpu.make_async_copy(keys.at[pl.ds(c * hh, hh)], kb.at[c, :, 0:tokens, :], k_sem)
    own_keys.start()

    def iota(shape, axis):
        return lax.broadcasted_iota(jnp.int32, shape, axis)

    page_of = jnp.where(slots[...] == iota((2 * hh, 128, 128), 1), 1.0, 0.0).astype(jnp.bfloat16)
    lane = iota((16, 128), 1)
    for hd in range(2 * hh):
        ids = picks[hd] + ncl
        used = jnp.zeros((16, 128), jnp.float32)
        for k in range(num_picks):
            used = jnp.where(ids[:, k : k + 1] == lane, 1.0, used)
        pages = lax.dot_general(used.astype(jnp.bfloat16), page_of[hd], NT, preferred_element_type=jnp.float32)
        coarse = jnp.where(jnp.logical_and(lane >= ncl, lane < 2 * ncl), 1.0 - used, 0.0)
        qx[hd // hh, hd % hh, 0:nq, :] = queries[hd]
        qx[hd // hh, hd % hh, nq : nq + 16, :] = (pages + coarse).astype(jnp.bfloat16)

    pl.semaphore_wait(barrier, 5 - 2 * first.astype(jnp.int32) - 2 * last.astype(jnp.int32))

    def q_out(way, half, h):
        chip = (z - 1, z, z + 1)[way]
        return copy(qx.at[half, h], qbuf.at[z, c, h], q_send.at[way, half, h], q_recv.at[z, c, h], chip, half)

    def q_hop(b, sc, h, chip):
        ref = qbuf.at[b, sc, h]
        return copy(ref, ref, f_send.at[b, sc, h], q_recv.at[b, sc, h], chip, c)

    def kv_out():
        return (
            copy(
                keys.at[pl.ds(o * hh, hh)], kb.at[c, :, 0:tokens, :], kv_send.at[0], kv_recv.at[0], z, o
            ),
            copy(cents.at[o], kb.at[c, :, tokens : tokens + 16, :], kv_send.at[2], kv_recv.at[2], z, o),
            copy(vx.at[o], vb.at[c], kv_send.at[1], kv_recv.at[1], z, o),
        )

    for h in range(hh // 2):

        @pl.when(jnp.logical_not(first))
        def _():
            for half in range(2):
                q_out(0, half, h).start()

        @pl.when(jnp.logical_not(last))
        def _():
            for half in range(2):
                q_out(2, half, h).start()

    for one in kv_out():
        one.start()

    for h in range(hh):
        q_out(1, o, h).start()

    kb[c, :, tokens : tokens + 16, :] = cents[c]
    vb[c] = vx[c]
    qbuf[z, c] = qx[c]
    wbuf[...] = jnp.zeros_like(wbuf)

    def tail_head(hd, carry):
        q = qx[hd // hh, hd % hh, 0:nq, :]
        s = lax.dot_general(nk[hd], q, NT, preferred_element_type=jnp.float32) * scale2
        shape = (num_steps * rows, nq)
        t, r = iota(shape, 0) // rows, iota(shape, 0) % rows
        lane = iota(shape, 1)
        seen = jnp.logical_and((lane // group) % rows == r, t <= lane // (rows * group))
        s = jnp.where(seen, s, floor2)
        top = jnp.max(s, axis=0, keepdims=True)
        w = jnp.where(seen, jnp.exp2(s - top), 0.0)
        tail_st[hd, 0:1, :] = top
        tail_st[hd, 1:2, :] = jnp.sum(w, axis=0, keepdims=True)
        tail[hd] = lax.dot_general(nv[hd], w.astype(jnp.bfloat16), TN, preferred_element_type=jnp.float32)
        return carry

    lax.fori_loop(0, 2 * hh, tail_head, 0)

    sel_rows = 48
    si, sl = iota((sel_rows, 128), 0), iota((sel_rows, 128), 1)
    in_page = si < 2 * cl
    blk = jnp.where(si >= 32, 1, 0)
    j = si - 16 - 16 * blk
    in_coarse = jnp.logical_and(si >= 16, j < cl)
    target = jnp.where(in_page, z * 2 * cl + si, jnp.where(in_coarse, ncl + (z * 2 + blk) * cl + j, -1))
    select = jnp.where(sl == target, 1.0, 0.0).astype(jnp.bfloat16)
    spread = jnp.where((iota((16, nq), 1) // group) % rows == iota((16, nq), 0), 1.0, 0.0).astype(jnp.bfloat16)

    own_keys.wait()
    for one in kv_out():
        one.wait_recv()

    def compute(b, sc, h):
        q = qbuf[b, sc, h, 0:nq, :]
        bits = qbuf[b, sc, h, nq : nq + 16, :]
        flags = lax.dot_general(select, bits, NT, preferred_element_type=jnp.float32)
        flags = jnp.dot(flags.astype(jnp.bfloat16), spread, preferred_element_type=jnp.float32)
        outs = []
        for d in range(2):
            score[d] = lax.dot_general(kb[d, h], q, NT, preferred_element_type=jnp.float32) * scale2
        for d in range(2):
            coarse_on = flags[16 + 16 * d : 32 + 16 * d, :] > 0.5
            coarse = score[d, tokens : tokens + 16, :] + coarse2
            top = jnp.max(jnp.where(coarse_on, coarse, floor2), axis=0, keepdims=True)
            on = [flags[d * cl + p : d * cl + p + 1, :] > 0.5 for p in range(cl)]
            for p in range(cl):
                page_top = jnp.max(score[d, p * page : (p + 1) * page, :], axis=0, keepdims=True)
                top = jnp.maximum(top, jnp.where(on[p], page_top, floor2))
            wc = jnp.where(coarse_on, jnp.exp2(coarse - top), 0.0)
            wbuf[d, tokens : tokens + 16, :] = wc.astype(jnp.bfloat16)
            total = jnp.sum(wc, axis=0, keepdims=True)
            for p in range(cl):
                w = jnp.exp2(score[d, p * page : (p + 1) * page, :] - jnp.where(on[p], top, 1e30))
                wbuf[d, p * page : (p + 1) * page, :] = w.astype(jnp.bfloat16)
                total = total + jnp.sum(w, axis=0, keepdims=True)
            outs.append((jnp.dot(vb[d, h, :, 0 : tokens + 16], wbuf[d, 0 : tokens + 16, :], preferred_element_type=jnp.float32), total, top))
        (o0, l0, m0), (o1, l1, m1) = outs
        top = jnp.maximum(m0, m1)
        a0, a1 = jnp.exp2(m0 - top), jnp.exp2(m1 - top)
        part[b, sc, h] = a0 * o0 + a1 * o1
        part_st[b, sc, h, 0:1, :] = top
        part_st[b, sc, h, 1:2, :] = a0 * l0 + a1 * l1

    def merge(o_ref, st_ref, values, st):
        m0, m1 = st_ref[0:1, :], st[0:1, :]
        top = jnp.maximum(m0, m1)
        a0, a1 = jnp.exp2(m0 - top), jnp.exp2(m1 - top)
        o_ref[...] = a0 * o_ref[...] + a1 * values
        st_ref[1:2, :] = a0 * st_ref[1:2, :] + a1 * st[1:2, :]
        st_ref[0:1, :] = top

    def decode(ref, st_ref):
        return ref[...].astype(jnp.int32).astype(jnp.float32) * st_ref[2:3, :]

    def flow_out(b, sc, h, chip, way):
        def hop(fn):
            fn(
                copy(snd.at[b, sc, h], inc.at[b, sc, h], s_send.at[0, b, sc, h], s_recv.at[0, b, sc, h], chip, c),
                copy(snd_st.at[b, sc, h], inc_st.at[b, sc, h], s_send.at[1, b, sc, h], s_recv.at[1, b, sc, h], chip, c),
            )

        def home(fn):
            fn(
                copy(snd.at[b, sc, h], fin.at[way, c, h], s_send.at[0, b, sc, h], f_recv.at[0, way, c, h], b, sc),
                copy(snd_st.at[b, sc, h], fin_st.at[way, c, h], s_send.at[1, b, sc, h], f_recv.at[1, way, c, h], b, sc),
            )

        return hop, home

    def both_start(x, y):
        x.start()
        y.start()

    def both_wait_send(x, y):
        x.wait_send()
        y.wait_send()

    def both_wait_recv(x, y):
        x.wait_recv()
        y.wait_recv()

    def sib_out(h):
        return (
            copy(part.at[z, o, h], sib.at[h], b_send.at[0, h], b_recv.at[0, h], z, o),
            copy(part_st.at[z, o, h], sib_st.at[h], b_send.at[1, h], b_recv.at[1, h], z, o),
        )

    def subslot(i):
        k = i % units
        side = k % 2
        place = jnp.where(side == 0, z, n - 1 - z)
        return i // units - 1, side, (k // 2 + c) % 2, k // 4, place

    def event(t, side, place):
        wave = jnp.where(t < place, 0, 1)
        dist = jnp.where(t < place, t + 1, 2 * place - t)
        valid = jnp.logical_and(t >= 0, t < 2 * place)
        return wave, jnp.clip(z + (2 * side - 1) * dist, 0, n - 1), valid

    def flow(bs, wave, side, sc, hw, place):
        @pl.when(jnp.logical_and(bs >= 0, bs < place))
        def _():
            bb = jnp.clip(jnp.where(side == 0, bs, n - 1 - bs), 0, n - 1)
            h = wave * (hh // 2) + hw
            o_ref, st_ref = part.at[bb, sc, h], part_st.at[bb, sc, h]

            @pl.when(place < n - 1)
            def _():
                flow_out(bb, sc, h, z, side)[0](both_wait_recv)
                merge(o_ref, st_ref, decode(inc.at[bb, sc, h], inc_st.at[bb, sc, h]), inc_st.at[bb, sc, h])

            values = o_ref[...]
            size = jnp.maximum(jnp.max(jnp.abs(values), axis=0, keepdims=True), 1e-30)
            snd[bb, sc, h] = jnp.round(values * (32767.0 / size)).astype(jnp.int32).astype(jnp.int16)
            snd_st[bb, sc, h, 0:2, :] = st_ref[0:2, :]
            snd_st[bb, sc, h, 2:3, :] = size * (1.0 / 32767.0)
            chip = z + 2 * side - 1
            hop, home = flow_out(bb, sc, h, chip, side)

            @pl.when(chip == bb)
            def _():
                home(both_start)

            @pl.when(chip != bb)
            def _():
                hop(both_start)

    def step(i, carry):
        t, side, sc, hw, place = subslot(i + units)
        wave, b, valid = event(t, side, place)
        h = wave * (hh // 2) + hw

        @pl.when(jnp.logical_and(valid, place < n - 1))
        def _():
            q_hop(b, sc, h, z).wait_recv()
            q_hop(b, sc, h, z + 1 - 2 * side).start()

        @pl.when(jnp.logical_and(jnp.logical_and(t == 2 * place, place < n - 1), sc == c))
        def _():
            @pl.when(side == 0)
            def _():
                for half in range(2):
                    q_out(2, half, hh // 2 + hw).start()

            @pl.when(side == 1)
            def _():
                for half in range(2):
                    q_out(0, half, hh // 2 + hw).start()

        t, side, sc, hw, place = subslot(i)
        wave, b, valid = event(t, side, place)
        early = jnp.logical_and(side == 0, sc == c)
        is_first, is_last = t == -1, t == 2 * n - 2
        own = jnp.logical_or(is_first, is_last)
        wave = jnp.where(own, side, wave)
        b = jnp.where(own, z, b)
        valid = jnp.where(is_first, early, jnp.where(is_last, jnp.logical_not(early), valid))
        h = wave * (hh // 2) + hw

        @pl.when(valid)
        def _():
            @pl.when(jnp.where(own, sc != c, place == n - 1))
            def _():
                q_hop(b, sc, h, z).wait_recv()

            compute(b, sc, h)

            @pl.when(jnp.logical_and(own, sc != c))
            def _():
                both_start(*sib_out(h))

        @pl.when(t >= 0)
        def _():
            def one(w, carry):
                bs = jnp.where(w == 0, 2 * n - 3 - place - t, t - 2 * n + 2 + place)
                flow(bs, w, side, sc, hw, place)
                return carry

            lax.fori_loop(0, 2, one, 0)

        return carry

    lax.fori_loop(0, 2 * n * units, step, 0)

    def finish(i, carry):
        half = (i % 2 + c) % 2
        h = i // 2
        hd = half * hh + h
        acc[...] = tail[hd]
        acc_st[...] = tail_st[hd]

        @pl.when(half == c)
        def _():
            merge(acc, acc_st, part[z, c, h], part_st.at[z, c, h])

        @pl.when(half != c)
        def _():
            both_wait_recv(*sib_out(h))
            merge(acc, acc_st, sib[h], sib_st.at[h])

        def arrive(way):
            both_wait_recv(
                copy(snd.at[0, 0, 0], fin.at[way, half, h], s_send.at[0, 0, 0, 0], f_recv.at[0, way, half, h], z, c),
                copy(snd_st.at[0, 0, 0], fin_st.at[way, half, h], s_send.at[1, 0, 0, 0], f_recv.at[1, way, half, h], z, c),
            )
            merge(acc, acc_st, decode(fin.at[way, half, h], fin_st.at[way, half, h]), fin_st.at[way, half, h])

        @pl.when(jnp.logical_not(last))
        def _():
            arrive(0)

        @pl.when(jnp.logical_not(first))
        def _():
            arrive(1)

        out[hd] = jnp.transpose(acc[...] / acc_st[1:2, :]).astype(jnp.bfloat16)
        return carry

    lax.fori_loop(0, units, finish, 0)

    for one in kv_out():
        one.wait_send()
    for h in range(hh):
        both_wait_send(*sib_out(h))
        q_out(1, o, h).wait_send()

        @pl.when(jnp.logical_not(first))
        def _():
            for half in range(2):
                q_out(0, half, h).wait_send()

        @pl.when(jnp.logical_not(last))
        def _():
            for half in range(2):
                q_out(2, half, h).wait_send()

    def drain(i, carry):
        b, sc, h = i // units, (i // hh) % 2, i % hh

        @pl.when(b != z)
        def _():
            flow_out(b, sc, h, z, 0)[0](both_wait_send)

            @pl.when(jnp.where(b < z, jnp.logical_not(last), jnp.logical_not(first)))
            def _():
                q_hop(b, sc, h, z).wait_send()

        return carry

    lax.fori_loop(0, n * units, drain, 0)


def per_device_paired(
    n,
    queries,
    new_keys,
    step_new_values,
    context_keys,
    context_values,
    cluster_centroid_keys,
    cluster_mean_values,
    cluster_page_slot,
    picks,
):
    num_steps, rows, num_heads, head_width = queries.shape
    kv_local, tokens = context_keys.shape[:2]
    cl = cluster_centroid_keys.shape[1]
    ncl = cluster_page_slot.shape[1]
    if 2 * ncl > 128 or rows > 16 or 2 * cl > 16 or kv_local % 4:
        return per_device_plain(
            queries, new_keys, step_new_values, context_keys, context_values,
            cluster_centroid_keys, cluster_mean_values, cluster_page_slot, picks,
        )
    page = tokens // cl
    group = num_heads // kv_local
    hh = kv_local // 2
    nq = num_steps * rows * group
    bf16, f32, i16 = jnp.bfloat16, jnp.float32, jnp.int16
    q = queries.reshape(num_steps, rows, kv_local, group, head_width)
    q = q.transpose(2, 0, 1, 3, 4).reshape(kv_local, nq, head_width)
    chosen = jnp.pad(picks.transpose(1, 0, 2), ((0, 0), (0, 16 - rows), (0, 0)), constant_values=-1)
    slots = jnp.pad(cluster_page_slot, ((0, 0), (ncl, 128 - 2 * ncl)), constant_values=-1)[:, None, :]
    pad = ((0, 0), (0, 16 - cl), (0, 0))
    cents = jnp.pad(cluster_centroid_keys, pad).reshape(2, hh, 16, head_width)
    pad = ((0, 0), (0, 128 - cl), (0, 0))
    vx = jnp.concatenate([context_values, jnp.pad(cluster_mean_values, pad)], axis=1)
    vx = vx.transpose(0, 2, 1).reshape(2, hh, head_width, tokens + 128)
    nk = new_keys.transpose(2, 0, 1, 3).reshape(kv_local, num_steps * rows, head_width)
    nv = step_new_values.transpose(2, 0, 1, 3).reshape(kv_local, num_steps * rows, head_width)
    dims = (num_steps, rows, group, hh, cl, page, head_width, ncl)
    dma = pltpu.SemaphoreType.DMA
    vm = pltpu.VMEM
    unit = (n, 2, hh)
    out = pl.pallas_call(
        functools.partial(chain_kernel, n, dims),
        out_shape=jax.ShapeDtypeStruct((kv_local, nq, head_width), bf16),
        in_specs=[pl.BlockSpec(memory_space=pltpu.VMEM)] * 8,
        out_specs=pl.BlockSpec(memory_space=pltpu.VMEM),
        scratch_shapes=[
            vm((2, hh, nq + 16, head_width), bf16),
            vm(unit + (nq + 16, head_width), bf16),
            vm((2, hh, tokens + 16, head_width), bf16),
            vm(vx.shape, bf16),
            vm(unit + (head_width, nq), f32),
            vm(unit + (4, nq), f32),
            vm(unit + (head_width, nq), i16),
            vm(unit + (4, nq), f32),
            vm(unit + (head_width, nq), i16),
            vm(unit + (4, nq), f32),
            vm((2, 2, hh, head_width, nq), i16),
            vm((2, 2, hh, 4, nq), f32),
            vm((hh, head_width, nq), f32),
            vm((hh, 4, nq), f32),
            vm((kv_local, head_width, nq), f32),
            vm((kv_local, 4, nq), f32),
            vm((head_width, nq), f32),
            vm((4, nq), f32),
            vm((2, tokens + 128, nq), bf16),
            vm((2, tokens + 16, nq), f32),
            dma((3, 2, hh)),
            dma(unit),
            dma(unit),
            dma((2,) + unit),
            dma((2,) + unit),
            dma((2, 2, 2, hh)),
            dma((2, hh)),
            dma((2, hh)),
            dma((3,)),
            dma((3,)),
            dma,
        ],
        compiler_params=pltpu.CompilerParams(
            collective_id=0, has_side_effects=True, vmem_limit_bytes=40 * 1024 * 1024
        ),
        cost_estimate=pl.CostEstimate(
            flops=8 * n * 2 * kv_local * nq * tokens * head_width,
            bytes_accessed=8 * 1024 * 1024,
            transcendentals=2 * n * kv_local * nq * tokens,
        ),
    )(q, context_keys, cents, vx, chosen, slots, nk, nv)
    out = out.reshape(kv_local, num_steps, rows, group, head_width)
    return out.transpose(1, 2, 0, 3, 4).reshape(num_steps, rows, num_heads, head_width)


def solution(mesh):
    sizes = mesh.shape
    paired = sizes["row"] == 1 and sizes["ctx"] % 2 == 0 and sizes["ctx"] > 2
    step = functools.partial(per_device_paired, sizes["ctx"] // 2) if paired else per_device_plain
    return jax.shard_map(
        step,
        mesh=mesh,
        in_specs=(
            P(None, ("groups", "ctx", "row"), "rep", None),
            P(None, ("groups", "ctx", "row"), "rep", None),
            P(None, ("groups", "ctx", "row"), "rep", None),
            P("rep", ("groups", "ctx"), None),
            P("rep", ("groups", "ctx"), None),
            P("rep", ("groups", "ctx"), None),
            P("rep", ("groups", "ctx"), None),
            P("rep", "groups"),
            P(("groups", "ctx", "row"), "rep", None),
        ),
        out_specs=P(None, ("groups", "ctx", "row"), "rep", None),
        check_vma=False,
    )
```
